128 devices in a mesh: slab: 4 (over x), pen: 32 (over z, y, core).
Axes of the slice: x: 4, y: 4, z: 4, core: 2. Of those that a mesh axis runs over, the one named last changes fastest.
Arguments:
- volume: bfloat16 [256, 128, 64, 128], P(None, 'pen', 'slab'), may hold values from -6 to 6
- occupancy: int32 [16, 8, 4], replicated, may hold values from 0 to 1, as said below
- gains: float32 [3, 128], replicated, may hold values from 0.5 to 1.5
- w_query: bfloat16 [3, 128, 128], replicated, as said below
- w_key: bfloat16 [3, 128, 128], replicated, as said below
- w_value: bfloat16 [3, 128, 128], replicated, may hold values from -0.5 to 0.5
- w_out: bfloat16 [3, 128, 128], replicated, may hold values from -0.5 to 0.5
Outputs:
- result: bfloat16 [256, 128, 64, 128], P(None, 'pen', 'slab')
The draws below stay inside these ranges and needn't reach their ends.
Inputs may be any that keep to these rules, and one draw needn't show every extreme that they name: `occupancy`: entries are 0 or 1; for every y-tile and z-tile index, each aligned group of 4 consecutive x-tiles holds exactly one occupied tile. `w_query`: entries lie within -24 / sqrt(128) and 24 / sqrt(128). `w_key`: entries lie within -24 / sqrt(128) and 24 / sqrt(128).
All inputs are finite; a program needn't handle non-finite values.
Results may differ from the reference program's by a relative error of at most 0.015.
Values may be sent and summed in bfloat16 or wider, within the bound.
No kernel may reach another device: no remote copies, remote signals or barrier semaphores. Data moves between devices by JAX's collectives and lax.ppermute only.
A program may use at most 128 MiB of HBM per device.

```python
import math
import jax
import jax.numpy as jnp
from jax import lax

D = 128
HEADS = 8
TILE = 16
NX = 256
NY = 128
NZ = 64


def scaled_normal(key, factor):
    base = jnp.clip(jax.random.normal(key, (3, D, D), jnp.float32), -4.0, 4.0)
    return base * (factor / math.sqrt(D))


def draw_w_query(key, part):
    key = jax.random.fold_in(key, 11)
    values = scaled_normal(key, 1.0)
    return values.astype(jnp.bfloat16)


def draw_w_key(key, part):
    key = jax.random.fold_in(key, 12)
    values = scaled_normal(key, 1.0)
    return values.astype(jnp.bfloat16)


def draw_occupancy(key, part):
    key = jax.random.fold_in(key, 13)
    groups = NX // TILE // 4
    tiles_y = NY // TILE
    tiles_z = NZ // TILE
    chosen = jax.random.randint(key, (groups, 1, tiles_y, tiles_z), 0, 4)
    slots = jnp.arange(4).astype(jnp.int32).reshape(1, 4, 1, 1)
    marks = (slots == chosen).astype(jnp.int32)
    return marks.reshape(groups * 4, tiles_y, tiles_z)


def level_of(key, shape, pieces, low, top_value):
    def one(position, blocks):
        draws = jax.random.uniform(jax.random.fold_in(jax.random.fold_in(key, 6), position), (blocks,), jnp.float32, low / len(pieces), top_value / len(pieces))
        return jnp.repeat(jnp.exp(draws), shape[position] // blocks).reshape((-1,) + (1,) * (len(shape) - position - 1))

    level = one(*pieces[0])
    for cut in pieces[1:]:
        level = level * one(*cut)
    return level


def normal_values(rng, extent, scale, limit, cuts=(), kind=jnp.bfloat16):
    values = jax.random.normal(rng, extent, jnp.float32) * scale
    if len(cuts) > 0:
        values = level_of(rng, extent, cuts, -0.22, 0.18) * values
    return jnp.clip(values, min=-limit, max=limit).astype(kind)


def setup_inputs(seed: int = 0) -> dict:
    keys = jax.random.split(jax.random.key(seed), 8)
    volume = normal_values(keys[0], (NX, NY, NZ, D), 1.0, 6.0, ((1, 32), (2, 4)))
    occupancy = draw_occupancy(jax.random.fold_in(keys[7], 71), 0)
    gains = jnp.clip(jax.random.uniform(keys[2], (3, D), jnp.float32, 0.5, 1.5), 0.5, 1.5)
    w_query = draw_w_query(jax.random.fold_in(keys[7], 71), 0)
    w_key = draw_w_key(jax.random.fold_in(keys[7], 71), 0)
    w_value = normal_values(keys[5], (3, D, D), D ** -0.5, 0.5)
    w_out = normal_values(keys[6], (3, D, D), D ** -0.5, 0.5)
    return dict(volume=volume, occupancy=occupancy, gains=gains, w_query=w_query, w_key=w_key, w_value=w_value, w_out=w_out)


def tile_mask(occupancy, counts):
    index_x = jnp.arange(counts[0]).astype(jnp.int32) // TILE
    index_y = jnp.arange(counts[1]).astype(jnp.int32) // TILE
    index_z = jnp.arange(counts[2]).astype(jnp.int32) // TILE
    picked = jnp.take(occupancy, index_x, axis=0)
    picked = jnp.take(picked, index_y, axis=1)
    return jnp.take(picked, index_z, axis=2)

def block_attend(rows_in, alive_mask, gain, w_query, w_key, w_value, w_out):
    count_lines, length, width = rows_in.shape
    head_size = width // HEADS
    widened = rows_in.astype(jnp.float32)
    row_mean = lax.optimization_barrier(jnp.mean(widened, axis=-1, keepdims=True))
    centred = widened - row_mean
    row_var = lax.optimization_barrier(jnp.mean(centred * centred, axis=-1, keepdims=True))
    normed = (centred * lax.rsqrt(row_var + 1e-05) * gain).astype(jnp.bfloat16)
    flat_rows = normed.reshape(count_lines * length, width)
    shaped = (count_lines, length, HEADS, head_size)
    query_rows = jnp.dot(flat_rows, w_query, preferred_element_type=jnp.float32).astype(jnp.bfloat16).reshape(shaped)
    key_rows = jnp.dot(flat_rows, w_key, preferred_element_type=jnp.float32).astype(jnp.bfloat16).reshape(shaped)
    value_rows = jnp.dot(flat_rows, w_value, preferred_element_type=jnp.float32).astype(jnp.bfloat16).reshape(shaped)
    scores = jnp.einsum('blhe,bmhe->bhlm', query_rows.astype(jnp.float32), key_rows.astype(jnp.float32)) * (1.0 / math.sqrt(head_size))
    live_keys = alive_mask[:, None, None, :] > 0
    scores = jnp.where(live_keys, scores, -1e+30)
    row_top = lax.optimization_barrier(jnp.max(scores, axis=-1, keepdims=True))
    exponent = jnp.exp(scores - row_top)
    row_total = lax.optimization_barrier(jnp.sum(exponent, axis=-1, keepdims=True))
    weights = (exponent / row_total).astype(jnp.bfloat16)
    attended = jnp.einsum('bhlm,bmhe->blhe', weights.astype(jnp.float32), value_rows.astype(jnp.float32)).astype(jnp.bfloat16)
    update = jnp.dot(attended.reshape(count_lines * length, width), w_out, preferred_element_type=jnp.float32).reshape(count_lines, length, width)
    update = jnp.where(alive_mask[:, :, None] > 0, update, 0.0)
    return (widened + update).astype(jnp.bfloat16)

def along_axis(volume, alive, axis, params):
    moved = jnp.moveaxis(volume, axis, -2)
    alive_moved = jnp.moveaxis(alive, axis, -1)
    length = moved.shape[-2]
    width = moved.shape[-1]
    line_count = moved.shape[0] * moved.shape[1]
    per_block = min(line_count, max(1, 2048 // length))
    grouped = moved.reshape(line_count // per_block, per_block, length, width)
    alive_grouped = alive_moved.reshape(line_count // per_block, per_block, length)

    def apply_block(packed):
        return block_attend(packed[0], packed[1], *params)
    result = lax.map(apply_block, (grouped, alive_grouped))
    result = result.reshape(moved.shape)
    return jnp.moveaxis(result, -2, axis)

def reference(volume, occupancy, gains, w_query, w_key, w_value, w_out):
    alive = tile_mask(occupancy, volume.shape[:3])
    for phase in range(3):
        params = (gains[phase], w_query[phase], w_key[phase], w_value[phase], w_out[phase])
        volume = along_axis(volume, alive, phase, params)
    return volume
```

```python
import functools
import math

import jax
import jax.numpy as jnp
from jax import lax
from jax.experimental import pallas as pl
from jax.experimental.pallas import tpu as pltpu
from jax.sharding import PartitionSpec as P

HEADS = 8
TILE = 16
GROUP = 4
BF16 = jnp.bfloat16
F32 = jnp.float32
BIG = 1e30
XU = 4
ZTS = 2
YTS = 2
GAP = 1
YIELD_AT = (1,3)
VMEM_BYTES = 48 * 2**20


def normalise(rows, gain):
    mean = jnp.mean(rows, axis=-1, keepdims=True)
    centred = rows - mean
    var = jnp.mean(centred * centred, axis=-1, keepdims=True)
    return (centred * lax.rsqrt(var + 1e-05) * gain).astype(BF16)


def dot_nt(a, b):
    return lax.dot_general(a, b, (((1,), (1,)), ((), ())), preferred_element_type=F32)


def dot_tn(a, b):
    return lax.dot_general(a, b, (((0,), (0,)), ((), ())), preferred_element_type=F32)


def dot_nn(a, b):
    return jnp.dot(a, b, preferred_element_type=F32)


def lane_of(width):
    return lax.broadcasted_iota(jnp.int32, (1, width), 1)


def ones_where(condition):
    return jnp.where(condition, 1.0, 0.0).astype(BF16)


def paired(weight):
    low = lane_of(128) < 64
    wide = weight.astype(F32)
    lo, hi = jnp.where(low, wide, 0.0), jnp.where(low, 0.0, wide)
    first = jnp.concatenate([lo, pltpu.roll(hi, 64, 1)], axis=1)
    second = jnp.concatenate([pltpu.roll(lo, 64, 1), hi], axis=1)
    return jnp.concatenate([first, second], axis=0).astype(BF16)


def placed(block, j, low):
    tile = block[:, (j // 2) * 128 : (j // 2 + 1) * 128] * low[j % 2]
    rest = jnp.zeros_like(tile)
    return jnp.concatenate([tile, rest] if j < 2 else [rest, tile], axis=1)


class Weights:
    def __init__(self, phase, gain_ref, w_query_ref, w_key_ref, w_value_ref, w_out_ref):
        self.gain = gain_ref[phase : phase + 1, :]
        self.query = paired(w_query_ref[phase])
        self.key = paired(w_key_ref[phase])
        self.value_t = w_value_ref[phase].astype(F32).T.astype(BF16)
        self.out = w_out_ref[phase]


def staggered(quads):
    results = [None] * len(quads)
    active, turn, started = [], 0, 0
    while active or started < len(quads):
        if started < len(quads) and turn % GAP == 0:
            active.append(started)
            started += 1
        for which in list(active):
            try:
                next(quads[which])
            except StopIteration as stop:
                results[which] = stop.value
                active.remove(which)
        turn += 1
    return sum(results, [])


def attend_quad(lines, weights, mask=None):
    length, width = lines[0].shape
    head_size = width // HEADS
    per_tile = 256 // length
    normed = normalise(jnp.concatenate(lines, axis=0), weights.gain)
    yield
    part = [normed[j * length : (j + 1) * length] for j in range(4)]
    beside = jnp.concatenate(
        [jnp.concatenate(part[0:2], axis=1), jnp.concatenate(part[2:4], axis=1)], axis=0
    )
    query = dot_nn(beside, weights.query).astype(BF16)
    key = dot_nn(beside, weights.key).astype(BF16)
    value_t = dot_nt(weights.value_t, normed).astype(BF16)
    yield
    lane = lane_of(256)
    halves = [ones_where(lane_of(128) // 64 == j) for j in range(2)]
    swap = (lane // 64) % 2 if length == 64 else 0
    head_masks = [ones_where((lane % 64) // head_size == (swap ^ i)) for i in range(4)]
    low = lane_of(128) < 64
    attended = [[] for _ in range(4)]

    def scores_of(half, t):
        lanes = slice(half * 128, (half + 1) * 128)
        query_half = jnp.concatenate([query[:length, lanes], query[length:, lanes]], axis=1)
        key_half = jnp.concatenate([key[:length, lanes], key[length:, lanes]], axis=1)
        key_rows = jnp.concatenate([placed(key_half, j, halves) for j in range(4)], axis=0)
        spread = jnp.concatenate(
            [query_half * head_masks[t * per_tile + i] for i in range(per_tile)], axis=0
        )
        return dot_nt(key_rows, spread)

    def weights_of(line):
        if mask is not None:
            line = line + mask
        top = jnp.max(line, axis=0, keepdims=True)
        line = jnp.exp2((line - top) * (math.log2(math.e) / math.sqrt(head_size)))
        return (line * (1.0 / jnp.sum(line, axis=0, keepdims=True))).astype(BF16)

    def gather(half, t, probs):
        if length == 64:
            values = value_t[half * 64 : (half + 1) * 64]
            lhs = jnp.concatenate([placed(values, j, halves) for j in range(4)], axis=0)
            out = dot_nn(lhs, jnp.concatenate(probs, axis=0))
            for i in range(4):
                at = slice((i // 2) * 128, (i // 2 + 1) * 128)
                for pair in range(2):
                    a = out[pair * 128 + i * 16 : pair * 128 + (i + 1) * 16, at]
                    b = out[pair * 128 + 64 + i * 16 : pair * 128 + 64 + (i + 1) * 16, at]
                    if i % 2:
                        attended[pair].append(pltpu.roll(jnp.where(low, b, a), 64, 1))
                    else:
                        attended[pair].append(jnp.where(low, a, b))
            return
        for pair in range(2):
            rows = slice(half * 64 + t * 32, half * 64 + (t + 1) * 32)
            values = value_t[rows, pair * 256 : (pair + 1) * 256]
            rest = jnp.zeros_like(values[:, :128])
            lhs = jnp.concatenate(
                [
                    jnp.concatenate([values[:, :128], rest], axis=1),
                    jnp.concatenate([rest, values[:, 128:]], axis=1),
                ],
                axis=0,
            )
            out = dot_nn(lhs, jnp.concatenate(probs[pair * 2 : pair * 2 + 2], axis=0))
            for j in range(2):
                for i in range(2):
                    attended[pair * 2 + j].append(
                        out[j * 32 + i * 16 : j * 32 + (i + 1) * 16, i * 128 : (i + 1) * 128]
                    )

    steps = [(half, t) for half in range(2) for t in range(4 // per_tile)]
    scores = scores_of(*steps[0])
    for k, step in enumerate(steps):
        yield
        ahead = scores_of(*steps[k + 1]) if k + 1 < len(steps) else None
        probs = []
        for j in range(4):
            probs.append(weights_of(scores[j * length : (j + 1) * length]))
            if j in YIELD_AT:
                yield
        gather(*step, probs)
        scores = ahead
    yield
    if length == 64:
        new = []
        for pair in range(2):
            joined = jnp.concatenate(attended[pair], axis=0).astype(BF16)
            update = dot_tn(joined, weights.out)
            new += [lines[pair * 2] + update[:64], lines[pair * 2 + 1] + update[64:]]
        return new
    return [
        lines[j] + dot_tn(jnp.concatenate(attended[j], axis=0).astype(BF16), weights.out)
        for j in range(4)
    ]


def label_of(occ_ref, group, tile_y, tile_z):
    label = jnp.int32(0)
    for k in range(1, GROUP):
        label = label + k * occ_ref[tile_y, tile_z, group * GROUP + k]
    return label


def x_kernel(occ_ref, vol_ref, *refs):
    given, (out_ref, res_ref, vin, whole, hs, sems, whole_sems) = refs[:5], refs[5:12]
    weight_refs, weight_sems = refs[12:17], refs[17]
    pen, slab = lax.axis_index("pen"), lax.axis_index("slab")
    tile_y = pen // 4
    loads = []
    for pair in range(2):
        for g in range(4):
            start = (g * GROUP + label_of(occ_ref, g, tile_y, slab)) * TILE
            loads.append(
                pltpu.make_async_copy(
                    vol_ref.at[pl.ds(start, TILE), pl.ds(pair * 2, 2)],
                    vin.at[pair, pl.ds(g * TILE, TILE)],
                    sems.at[pair, g],
                )
            )
            loads[-1].start()
        if pair == 0:
            for k in range(5):
                loads.append(pltpu.make_async_copy(given[k], weight_refs[k], weight_sems.at[k]))
                loads[-1].start()
    fetch = pltpu.make_async_copy(vol_ref, whole, whole_sems.at[0])
    store = pltpu.make_async_copy(whole, res_ref, whole_sems.at[1])
    fetch.start()
    for copy in loads:
        copy.wait()
    weights = Weights(0, *weight_refs)

    def pair_step(pair, carry):
        hs[...] = vin[pair].astype(F32).reshape(64 * 32, 128)

        def step(i, inner):
            at = i * (4 * XU)
            lines = [hs[pl.ds(at + j, 64, stride=32), :] for j in range(4 * XU)]
            new = staggered([attend_quad(lines[4 * u : 4 * u + 4], weights) for u in range(XU)])
            for j in range(4 * XU):
                hs[pl.ds(at + j, 64, stride=32), :] = new[j]
            return inner

        lax.fori_loop(0, 8 // XU, step, 0)
        done = hs[...].reshape(64, 2, 2, 8, 128)
        rows = pl.ds(pl.multiple_of(pair * 16, 16), 16)
        for half in range(2):
            out_ref[:, half, rows] = done[:, :, half].reshape(64, 16, 128).astype(BF16)

        @pl.when(pair == 0)
        def _():
            fetch.wait()
            store.start()

        return carry

    lax.fori_loop(0, 2, pair_step, 0)
    store.wait()


def same_tile_mask(labels, repeat):
    tokens = TILE * len(labels)
    tile = lax.broadcasted_iota(jnp.int32, (1, tokens), 1) // TILE
    queries = jnp.zeros((1, tokens), jnp.int32)
    for t, label in enumerate(labels):
        queries = jnp.where(tile == t, label, queries)
    queries = jnp.concatenate([queries] * repeat, axis=1)
    rows = [
        jnp.broadcast_to(jnp.where(queries == label, 0.0, -BIG), (TILE, tokens * repeat))
        for label in labels
    ]
    return jnp.concatenate(rows, axis=0)


def y_kernel(occ_ref, in_ref, *refs):
    weight_refs, (keep_ref, send_ref, hs) = refs[:5], refs[5:]
    pen, slab = lax.axis_index("pen"), lax.axis_index("slab")
    core = pen % 2
    first = pl.program_id(0) * ZTS
    hs[...] = in_ref[...].astype(F32).reshape(ZTS * 1024, 128)
    weights = Weights(1, *weight_refs)
    masks = [
        same_tile_mask([label_of(occ_ref, slab, t, first + k) for t in range(8)], 2)
        for k in range(ZTS)
    ]
    places = [pl.ds(k * 1024 + z, 128, stride=8) for k in range(ZTS) for z in range(8)]
    lines = [hs[at, :] for at in places]
    new = staggered(
        [attend_quad(lines[4 * u : 4 * u + 4], weights, masks[u // 2]) for u in range(2 * ZTS)]
    )
    for at, line in zip(places, new):
        hs[at, :] = line
    for k in range(ZTS):
        for p in range(32):
            base = k * 1024 + p * 32
            keep = pl.ds(pl.multiple_of(base + core * 16, 16), 16)
            send = pl.ds(pl.multiple_of(base + 16 - core * 16, 16), 16)
            keep_ref[k, p] = hs[keep, :].astype(BF16)
            send_ref[k, p] = hs[send, :].astype(BF16)


def z_kernel(occ_ref, kept_ref, got_ref, *refs):
    weight_refs, (out_ref,) = refs[:5], refs[5:]
    pen, slab = lax.axis_index("pen"), lax.axis_index("slab")
    first = pen % 2 == 0
    weights = Weights(2, *weight_refs)

    def step(i, carry):
        masks = [
            same_tile_mask([label_of(occ_ref, slab, i * YTS + k, t) for t in range(4)], 4)
            for k in range(YTS)
        ]
        base = i * (4 * YTS)
        lines = []
        for u in range(4 * YTS):
            pair = ([], [])
            for t in range(4):
                for ref in (kept_ref, got_ref):
                    both = ref[t, base + u].astype(F32)
                    pair[0].append(both[:8])
                    pair[1].append(both[8:])
            lines += [jnp.concatenate(pair[0], axis=0), jnp.concatenate(pair[1], axis=0)]
        new = staggered(
            [attend_quad(lines[4 * u : 4 * u + 4], weights, masks[u // 2]) for u in range(2 * YTS)]
        )
        for j in range(8 * YTS):
            for t in range(4):
                kept, got = new[j][t * 16 : t * 16 + 8], new[j][t * 16 + 8 : t * 16 + 16]
                ordered = jnp.concatenate(
                    [jnp.where(first, kept, got), jnp.where(first, got, kept)], axis=0
                )
                rows = slice((j % 2) * 16, (j % 2 + 1) * 16)
                out_ref[t * 32 + base + j // 2, rows, :] = ordered.astype(BF16)
        return carry

    lax.fori_loop(0, 8 // YTS, step, 0)


def merge_kernel(occ_ref, new_ref, res_in_ref, res_ref, sems):
    del res_in_ref
    pen, slab = lax.axis_index("pen"), lax.axis_index("slab")
    tile_y = pen // 4
    copies = []
    for g in range(4):
        start = (g * GROUP + label_of(occ_ref, g, tile_y, slab)) * TILE
        for k in range(4):
            copies.append(
                pltpu.make_async_copy(
                    new_ref.at[pl.ds(g * TILE + k * 4, 4)],
                    res_ref.at[pl.ds(start + k * 4, 4)],
                    sems.at[g * 4 + k],
                )
            )
            copies[-1].start()
    for copy in copies:
        copy.wait()


SMEM = pl.BlockSpec(memory_space=pltpu.SMEM)
VMEM = pl.BlockSpec(memory_space=pltpu.VMEM)
ANY = pl.BlockSpec(memory_space=pl.ANY)
HBM = pl.BlockSpec(memory_space=pltpu.HBM)
PARAMS = pltpu.CompilerParams(vmem_limit_bytes=VMEM_BYTES)


def body(volume, occupancy, gains, w_query, w_key, w_value, w_out):
    params = (gains, w_query, w_key, w_value, w_out)
    occupancy = jnp.transpose(occupancy, (1, 2, 0))
    after_x, copied = pl.pallas_call(
        x_kernel,
        out_shape=(
            jax.ShapeDtypeStruct((64, 2, 32, 128), BF16),
            jax.ShapeDtypeStruct(volume.shape, BF16),
        ),
        in_specs=[SMEM, HBM, *[HBM] * 5],
        out_specs=(VMEM, HBM),
        scratch_shapes=[
            pltpu.VMEM((2, 64, 2, 16, 128), BF16),
            pltpu.VMEM(volume.shape, BF16),
            pltpu.VMEM((64 * 32, 128), F32),
            pltpu.SemaphoreType.DMA((2, 4)),
            pltpu.SemaphoreType.DMA((2,)),
            *[pltpu.VMEM(array.shape, array.dtype) for array in params],
            pltpu.SemaphoreType.DMA((5,)),
        ],
        compiler_params=pltpu.CompilerParams(vmem_limit_bytes=60 * 2**20),
        name="x_phase",
    )(occupancy, volume, *params)

    both = ("slab", "pen")
    planes = lax.all_to_all(after_x.reshape(128, 32, 128), both, 0, 0, tiled=True)

    half = jax.ShapeDtypeStruct((4, 32, 16, 128), BF16)
    half_spec = pl.BlockSpec((ZTS, 32, 16, 128), lambda i: (i, 0, 0, 0))
    kept, sent = pl.pallas_call(
        y_kernel,
        grid=(4 // ZTS,),
        out_shape=(half, half),
        in_specs=[SMEM, pl.BlockSpec((32 * ZTS, 32, 128), lambda i: (i, 0, 0)), *[VMEM] * 5],
        out_specs=(half_spec, half_spec),
        scratch_shapes=[pltpu.VMEM((ZTS * 1024, 128), F32)],
        compiler_params=PARAMS,
        name="y_phase",
    )(occupancy, planes, *params)

    got = lax.ppermute(sent, "pen", [(p, p ^ 1) for p in range(lax.axis_size("pen"))])

    after_z = pl.pallas_call(
        z_kernel,
        out_shape=jax.ShapeDtypeStruct((128, 32, 128), BF16),
        in_specs=[SMEM, VMEM, VMEM, *[VMEM] * 5],
        out_specs=VMEM,
        compiler_params=PARAMS,
        name="z_phase",
    )(occupancy, kept, got, *params)

    home = lax.all_to_all(after_z, both, 0, 0, tiled=True).reshape(64, 4, 16, 128)

    return pl.pallas_call(
        merge_kernel,
        out_shape=jax.ShapeDtypeStruct(volume.shape, BF16),
        in_specs=[SMEM, ANY, HBM],
        out_specs=HBM,
        scratch_shapes=[pltpu.SemaphoreType.DMA((16,))],
        input_output_aliases={2: 0},
        compiler_params=PARAMS,
        name="merge",
    )(occupancy, home, copied)


def solution(mesh):
    placed = (P(None, "pen", "slab", None), P(), P(), P(), P(), P(), P())
    return jax.shard_map(
        body, mesh=mesh, in_specs=placed, out_specs=P(None, "pen", "slab", None), check_vma=False
    )
```

```python
import functools
import math

import jax
import jax.numpy as jnp
from jax import lax
from jax.experimental import pallas as pl
from jax.experimental.pallas import tpu as pltpu
from jax.sharding import PartitionSpec as P

HEADS = 8
TILE = 16
GROUP = 4
BF16 = jnp.bfloat16
F32 = jnp.float32
BIG = 1e30
Y_STRIDE = 9
STRIDE = 36
XU = 8
YTS = 4
GAP = 1
YIELD_AT = (1,3)
VMEM_BYTES = 48 * 2**20


def normalise(rows, gain):
    mean = jnp.mean(rows, axis=-1, keepdims=True)
    centred = rows - mean
    var = jnp.mean(centred * centred, axis=-1, keepdims=True)
    return (centred * lax.rsqrt(var + 1e-05) * gain).astype(BF16)


def dot_nt(a, b):
    return lax.dot_general(a, b, (((1,), (1,)), ((), ())), preferred_element_type=F32)


def dot_tn(a, b):
    return lax.dot_general(a, b, (((0,), (0,)), ((), ())), preferred_element_type=F32)


def dot_nn(a, b):
    return jnp.dot(a, b, preferred_element_type=F32)


def lane_of(width):
    return lax.broadcasted_iota(jnp.int32, (1, width), 1)


def ones_where(condition):
    return jnp.where(condition, 1.0, 0.0).astype(BF16)


def paired(weight):
    low = lane_of(128) < 64
    wide = weight.astype(F32)
    lo, hi = jnp.where(low, wide, 0.0), jnp.where(low, 0.0, wide)
    first = jnp.concatenate([lo, pltpu.roll(hi, 64, 1)], axis=1)
    second = jnp.concatenate([pltpu.roll(lo, 64, 1), hi], axis=1)
    return jnp.concatenate([first, second], axis=0).astype(BF16)


def placed(block, j, low):
    tile = block[:, (j // 2) * 128 : (j // 2 + 1) * 128] * low[j % 2]
    rest = jnp.zeros_like(tile)
    return jnp.concatenate([tile, rest] if j < 2 else [rest, tile], axis=1)


class Weights:
    def __init__(self, phase, gain_ref, w_query_ref, w_key_ref, w_value_ref, w_out_ref):
        self.gain = gain_ref[phase : phase + 1, :]
        self.query = paired(w_query_ref[phase])
        self.key = paired(w_key_ref[phase])
        self.value_t = w_value_ref[phase].astype(F32).T.astype(BF16)
        self.out = w_out_ref[phase]


def staggered(quads):
    results = [None] * len(quads)
    active, turn, started = [], 0, 0
    while active or started < len(quads):
        if started < len(quads) and turn % GAP == 0:
            active.append(started)
            started += 1
        for which in list(active)[::-1]:
            try:
                next(quads[which])
            except StopIteration as stop:
                results[which] = stop.value
                active.remove(which)
        turn += 1
    return sum(results, [])


def attend_quad(lines, weights, mask=None):
    length, width = lines[0].shape
    head_size = width // HEADS
    per_tile = 256 // length
    normed = normalise(jnp.concatenate(lines, axis=0), weights.gain)
    yield
    part = [normed[j * length : (j + 1) * length] for j in range(4)]
    beside = jnp.concatenate(
        [jnp.concatenate(part[0:2], axis=1), jnp.concatenate(part[2:4], axis=1)], axis=0
    )
    query = dot_nn(beside, weights.query).astype(BF16)
    key = dot_nn(beside, weights.key).astype(BF16)
    value_t = dot_nt(weights.value_t, normed).astype(BF16)
    yield
    lane = lane_of(256)
    halves = [ones_where(lane_of(128) // 64 == j) for j in range(2)]
    swap = (lane // 64) % 2 if length == 64 else 0
    head_masks = [ones_where((lane % 64) // head_size == (swap ^ i)) for i in range(4)]
    low = lane_of(128) < 64
    attended = [[] for _ in range(4)]

    def scores_of(half, t):
        lanes = slice(half * 128, (half + 1) * 128)
        query_half = jnp.concatenate([query[:length, lanes], query[length:, lanes]], axis=1)
        key_half = jnp.concatenate([key[:length, lanes], key[length:, lanes]], axis=1)
        key_rows = jnp.concatenate([placed(key_half, j, halves) for j in range(4)], axis=0)
        spread = jnp.concatenate(
            [query_half * head_masks[t * per_tile + i] for i in range(per_tile)], axis=0
        )
        return dot_nt(key_rows, spread)

    def weights_of(line):
        if mask is not None:
            line = line + mask
        top = jnp.max(line, axis=0, keepdims=True)
        line = jnp.exp2((line - top) * (math.log2(math.e) / math.sqrt(head_size)))
        return (line * (1.0 / jnp.sum(line, axis=0, keepdims=True))).astype(BF16)

    def gather(half, t, probs):
        if length == 64:
            values = value_t[half * 64 : (half + 1) * 64]
            lhs = jnp.concatenate([placed(values, j, halves) for j in range(4)], axis=0)
            out = dot_nn(lhs, jnp.concatenate(probs, axis=0))
            for i in range(4):
                at = slice((i // 2) * 128, (i // 2 + 1) * 128)
                for pair in range(2):
                    a = out[pair * 128 + i * 16 : pair * 128 + (i + 1) * 16, at]
                    b = out[pair * 128 + 64 + i * 16 : pair * 128 + 64 + (i + 1) * 16, at]
                    if i % 2:
                        attended[pair].append(pltpu.roll(jnp.where(low, b, a), 64, 1))
                    else:
                        attended[pair].append(jnp.where(low, a, b))
            return
        for pair in range(2):
            rows = slice(half * 64 + t * 32, half * 64 + (t + 1) * 32)
            values = value_t[rows, pair * 256 : (pair + 1) * 256]
            rest = jnp.zeros_like(values[:, :128])
            lhs = jnp.concatenate(
                [
                    jnp.concatenate([values[:, :128], rest], axis=1),
                    jnp.concatenate([rest, values[:, 128:]], axis=1),
                ],
                axis=0,
            )
            out = dot_nn(lhs, jnp.concatenate(probs[pair * 2 : pair * 2 + 2], axis=0))
            for j in range(2):
                for i in range(2):
                    attended[pair * 2 + j].append(
                        out[j * 32 + i * 16 : j * 32 + (i + 1) * 16, i * 128 : (i + 1) * 128]
                    )

    steps = [(half, t) for half in range(2) for t in range(4 // per_tile)]
    scores = scores_of(*steps[0])
    for k, step in enumerate(steps):
        yield
        ahead = scores_of(*steps[k + 1]) if k + 1 < len(steps) else None
        probs = []
        for j in range(4):
            probs.append(weights_of(scores[j * length : (j + 1) * length]))
            if j in YIELD_AT:
                yield
        gather(*step, probs)
        yield
        scores = ahead
    yield
    if length == 64:
        new = []
        for pair in range(2):
            joined = jnp.concatenate(attended[pair], axis=0).astype(BF16)
            update = dot_tn(joined, weights.out)
            new += [lines[pair * 2] + update[:64], lines[pair * 2 + 1] + update[64:]]
        return new
    return [
        lines[j] + dot_tn(jnp.concatenate(attended[j], axis=0).astype(BF16), weights.out)
        for j in range(4)
    ]


def label_of(occ_ref, group, tile_y, tile_z):
    label = jnp.int32(0)
    for k in range(1, GROUP):
        label = label + k * occ_ref[tile_y, tile_z, group * GROUP + k]
    return label


def x_kernel(occ_ref, vol_ref, *refs):
    given, (out_ref, res_ref, vin, whole, hs, done, sems, whole_sems, out_sems) = refs[:5], refs[5:14]
    weight_refs, weight_sems = refs[14:19], refs[19]
    chip, slab = lax.axis_index("chip"), lax.axis_index("slab")
    tile_y = chip // 2
    tiles = []
    for pair in range(2):
        for g in range(4):
            start = (g * GROUP + label_of(occ_ref, g, tile_y, slab)) * TILE
            tiles.append(
                pltpu.make_async_copy(
                    vol_ref.at[pl.ds(start, TILE), pl.ds(pair * 2, 2)],
                    vin.at[pair, pl.ds(g * TILE, TILE)],
                    sems.at[pair, g],
                )
            )
    fetch = pltpu.make_async_copy(vol_ref, whole, whole_sems.at[0])
    store = pltpu.make_async_copy(whole, res_ref, whole_sems.at[1])
    weight_loads = [
        pltpu.make_async_copy(given[k], weight_refs[k], weight_sems.at[k]) for k in range(5)
    ]
    for copy in tiles[:4] + weight_loads + tiles[4:]:
        copy.start()
    for copy in weight_loads:
        copy.wait()
    weights = Weights(0, *weight_refs)
    for copy in tiles[:4]:
        copy.wait()
    outs = []
    for pair in range(2):
        if pair:
            for copy in tiles[4:]:
                copy.wait()
            fetch.wait()
            store.start()
        held = hs.reshape(64, STRIDE, 128)
        held[:, :32, :] = vin[pair].astype(F32).reshape(64, 32, 128)
        if pair == 0:
            fetch.start()

        def step(i, inner):
            at = i * (4 * XU)
            lines = [hs[pl.ds(at + j, 64, stride=STRIDE), :] for j in range(4 * XU)]
            new = staggered([attend_quad(lines[4 * u : 4 * u + 4], weights) for u in range(XU)])
            for j in range(4 * XU):
                hs[pl.ds(at + j, 64, stride=STRIDE), :] = new[j]
            return inner

        lax.fori_loop(0, 8 // XU, step, 0)
        split = held[:, :32, :].reshape(64, 2, 2, 8, 128)
        for half in range(2):
            done[pair, half] = split[:, :, half].reshape(64, 16, 128).astype(BF16)
        outs.append(
            pltpu.make_async_copy(
                done.at[pair], out_ref.at[:, :, pl.ds(pair * 16, 16)], out_sems.at[pair]
            )
        )
        outs[-1].start()
    for copy in [store, *outs]:
        copy.wait()


def same_tile_mask(labels, repeat):
    tokens = TILE * len(labels)
    tile = lax.broadcasted_iota(jnp.int32, (1, tokens), 1) // TILE
    queries = jnp.zeros((1, tokens), jnp.int32)
    for t, label in enumerate(labels):
        queries = jnp.where(tile == t, label, queries)
    queries = jnp.concatenate([queries] * repeat, axis=1)
    rows = [
        jnp.broadcast_to(jnp.where(queries == label, 0.0, -BIG), (TILE, tokens * repeat))
        for label in labels
    ]
    return jnp.concatenate(rows, axis=0)


def y_kernel(occ_ref, in_ref, *refs):
    weight_refs, (keep_ref, send_ref, hs) = refs[:5], refs[5:]
    chip, slab = lax.axis_index("chip"), lax.axis_index("slab")
    core = lax.axis_index("core")
    held = hs.reshape(4, 16, 2, 4, Y_STRIDE, 128)
    for side in range(2):
        held[:, :, side, :, :8, :] = in_ref[side].astype(F32).reshape(4, 16, 4, 8, 128)
    weights = Weights(1, *weight_refs)
    masks = [
        same_tile_mask([label_of(occ_ref, slab, t, tile_z) for t in range(8)], 2)
        for tile_z in range(4)
    ]
    places = [
        pl.ds(k * 128 * Y_STRIDE + z, 128, stride=Y_STRIDE) for k in range(4) for z in range(8)
    ]
    lines = [hs[at, :] for at in places]
    new = staggered(
        [attend_quad(lines[4 * u : 4 * u + 4], weights, masks[u // 2]) for u in range(8)]
    )
    for at, line in zip(places, new):
        hs[at, :] = line
    for k in range(4):
        for p in range(32):
            for ref, side in ((keep_ref, core), (send_ref, 1 - core)):
                rows = [held[k, p // 2, p % 2, side * 2 + j, :8, :] for j in range(2)]
                ref[k, p] = jnp.concatenate(rows, axis=0).astype(BF16)


def z_kernel(occ_ref, kept_ref, got_ref, *refs):
    weight_refs, (out_ref,) = refs[:5], refs[5:]
    chip, slab = lax.axis_index("chip"), lax.axis_index("slab")
    first = lax.axis_index("core") == 0
    weights = Weights(2, *weight_refs)

    def step(i, carry):
        masks = [
            same_tile_mask([label_of(occ_ref, slab, i * YTS + k, t) for t in range(4)], 4)
            for k in range(YTS)
        ]
        base = i * (4 * YTS)
        lines = []
        for u in range(4 * YTS):
            pair = ([], [])
            for t in range(4):
                for ref in (kept_ref, got_ref):
                    both = ref[t, base + u].astype(F32)
                    pair[0].append(both[:8])
                    pair[1].append(both[8:])
            lines += [jnp.concatenate(pair[0], axis=0), jnp.concatenate(pair[1], axis=0)]
        new = staggered(
            [attend_quad(lines[4 * u : 4 * u + 4], weights, masks[u // 2]) for u in range(2 * YTS)]
        )
        for j in range(8 * YTS):
            for t in range(4):
                kept, got = new[j][t * 16 : t * 16 + 8], new[j][t * 16 + 8 : t * 16 + 16]
                ordered = jnp.concatenate(
                    [jnp.where(first, kept, got), jnp.where(first, got, kept)], axis=0
                )
                rows = slice((j % 2) * 16, (j % 2 + 1) * 16)
                u = j // 2
                out_ref[u % 2, t * 16 + base // 2 + u // 2, rows, :] = ordered.astype(BF16)
        return carry

    lax.fori_loop(0, 8 // YTS, step, 0)


def merge_kernel(occ_ref, new_ref, res_in_ref, res_ref, sems):
    del res_in_ref
    chip, slab = lax.axis_index("chip"), lax.axis_index("slab")
    tile_y = chip // 2
    copies = []
    for g in range(4):
        start = (g * GROUP + label_of(occ_ref, g, tile_y, slab)) * TILE
        for side in range(2):
            copies.append(
                pltpu.make_async_copy(
                    new_ref.at[side, pl.ds(g * TILE, TILE)],
                    res_ref.at[pl.ds(start, TILE), pl.ds(side * 2, 2)],
                    sems.at[g * 2 + side],
                )
            )
            copies[-1].start()
    for copy in copies:
        copy.wait()


SMEM = pl.BlockSpec(memory_space=pltpu.SMEM)
VMEM = pl.BlockSpec(memory_space=pltpu.VMEM)
ANY = pl.BlockSpec(memory_space=pl.ANY)
HBM = pl.BlockSpec(memory_space=pltpu.HBM)
PARAMS = pltpu.CompilerParams(vmem_limit_bytes=VMEM_BYTES)


def body(volume, occupancy, gains, w_query, w_key, w_value, w_out):
    params = (gains, w_query, w_key, w_value, w_out)
    occupancy = jnp.transpose(occupancy, (1, 2, 0))
    after_x, copied = pl.pallas_call(
        x_kernel,
        out_shape=(
            jax.ShapeDtypeStruct((2, 64, 32, 128), BF16),
            jax.ShapeDtypeStruct(volume.shape, BF16),
        ),
        in_specs=[SMEM, HBM, *[HBM] * 5],
        out_specs=(HBM, HBM),
        scratch_shapes=[
            pltpu.VMEM((2, 64, 2, 16, 128), BF16),
            pltpu.VMEM(volume.shape, BF16),
            pltpu.VMEM((64 * STRIDE, 128), F32),
            pltpu.VMEM((2, 2, 64, 16, 128), BF16),
            pltpu.SemaphoreType.DMA((2, 4)),
            pltpu.SemaphoreType.DMA((2,)),
            pltpu.SemaphoreType.DMA((2,)),
            *[pltpu.VMEM(array.shape, array.dtype) for array in params],
            pltpu.SemaphoreType.DMA((5,)),
        ],
        compiler_params=pltpu.CompilerParams(vmem_limit_bytes=60 * 2**20),
        name="x_phase",
    )(occupancy, volume, *params)

    every = ("core", "slab", "chip")
    planes = lax.all_to_all(after_x.reshape(128, 32, 128), every, 0, 0, tiled=True)

    half = jax.ShapeDtypeStruct((4, 32, 16, 128), BF16)
    kept, sent = pl.pallas_call(
        y_kernel,
        out_shape=(half, half),
        in_specs=[SMEM, VMEM, *[VMEM] * 5],
        out_specs=(VMEM, VMEM),
        scratch_shapes=[pltpu.VMEM((4 * 128 * Y_STRIDE, 128), F32)],
        compiler_params=PARAMS,
        name="y_phase",
    )(occupancy, planes.reshape(2, 64, 32, 128), *params)

    got = lax.ppermute(sent, "core", [(0, 1), (1, 0)])

    after_z = pl.pallas_call(
        z_kernel,
        out_shape=jax.ShapeDtypeStruct((2, 64, 32, 128), BF16),
        in_specs=[SMEM, VMEM, VMEM, *[VMEM] * 5],
        out_specs=VMEM,
        compiler_params=PARAMS,
        name="z_phase",
    )(occupancy, kept, got, *params)

    home = lax.all_to_all(after_z.reshape(128, 32, 128), every, 0, 0, tiled=True)

    return pl.pallas_call(
        merge_kernel,
        out_shape=jax.ShapeDtypeStruct(volume.shape, BF16),
        in_specs=[SMEM, ANY, HBM],
        out_specs=HBM,
        scratch_shapes=[pltpu.SemaphoreType.DMA((8,))],
        input_output_aliases={2: 0},
        compiler_params=PARAMS,
        name="merge",
    )(occupancy, home.reshape(2, 64, 2, 16, 128), copied)


def solution(mesh):
    devices = mesh.devices.reshape(mesh.shape["slab"], -1, 2)
    cores = jax.sharding.Mesh(devices, ("slab", "chip", "core"))
    volume = P(None, ("chip", "core"), "slab", None)
    placed = (volume, P(), P(), P(), P(), P(), P())
    return jax.shard_map(body, mesh=cores, in_specs=placed, out_specs=volume, check_vma=False)
```

```python
import functools
import math

import jax
import jax.numpy as jnp
from jax import lax
from jax.experimental import pallas as pl
from jax.experimental.pallas import tpu as pltpu
from jax.sharding import PartitionSpec as P

HEADS = 8
TILE = 16
GROUP = 4
BF16 = jnp.bfloat16
F32 = jnp.float32
BIG = 1e30
Y_STRIDE = 9
STRIDE = 36
GAP = 1
VMEM_BYTES = 48 * 2**20


def normalise(rows, gain):
    width = rows.shape[1]
    centred = rows - jnp.sum(rows, axis=-1, keepdims=True) * (1.0 / width)
    total = jnp.sum(centred * centred, axis=-1, keepdims=True)
    return (centred * lax.rsqrt(total + 1e-05 * width) * gain).astype(BF16)


def dot_nt(a, b):
    return lax.dot_general(a, b, (((1,), (1,)), ((), ())), preferred_element_type=F32)


def dot_tn(a, b):
    return lax.dot_general(a, b, (((0,), (0,)), ((), ())), preferred_element_type=F32)


def dot_nn(a, b):
    return jnp.dot(a, b, preferred_element_type=F32)


def lane_of(width):
    return lax.broadcasted_iota(jnp.int32, (1, width), 1)


def ones_where(condition):
    return jnp.where(condition, 1.0, 0.0).astype(BF16)


def paired(weight):
    low = lane_of(128) < 64
    wide = weight.astype(F32)
    lo, hi = jnp.where(low, wide, 0.0), jnp.where(low, 0.0, wide)
    first = jnp.concatenate([lo, pltpu.roll(hi, 64, 1)], axis=1)
    second = jnp.concatenate([pltpu.roll(lo, 64, 1), hi], axis=1)
    return jnp.concatenate([first, second], axis=0).astype(BF16)


def placed(block, j, low):
    tile = block[:, (j // 2) * 128 : (j // 2 + 1) * 128] * low[j % 2]
    rest = jnp.zeros_like(tile)
    return jnp.concatenate([tile, rest] if j < 2 else [rest, tile], axis=1)


class Weights:
    def __init__(self, phase, gain_ref, w_query_ref, w_key_ref, w_value_ref, w_out_ref):
        self.gain = gain_ref[phase : phase + 1, :] * math.sqrt(128)
        self.query = paired(w_query_ref[phase])
        self.key = paired(w_key_ref[phase])
        self.value_t = w_value_ref[phase].astype(F32).T.astype(BF16)
        self.out = w_out_ref[phase]


def staggered(quads):
    results = [None] * len(quads)
    active, turn, started = [], 0, 0
    while active or started < len(quads):
        if started < len(quads) and turn % GAP == 0:
            active.append(started)
            started += 1
        for which in list(active)[::-1]:
            try:
                next(quads[which])
            except StopIteration as stop:
                results[which] = stop.value
                active.remove(which)
        turn += 1
    return sum(results, [])


def attend_quad(lines, weights, mask=None):
    length, width = lines[0].shape
    head_size = width // HEADS
    per_tile = 256 // length
    normed = normalise(jnp.concatenate(lines, axis=0), weights.gain)
    yield
    part = [normed[j * length : (j + 1) * length] for j in range(4)]
    beside = jnp.concatenate(
        [jnp.concatenate(part[0:2], axis=1), jnp.concatenate(part[2:4], axis=1)], axis=0
    )
    query = dot_nn(beside, weights.query).astype(BF16)
    key = dot_nn(beside, weights.key).astype(BF16)
    value_t = dot_nt(weights.value_t, normed).astype(BF16)
    yield
    lane = lane_of(256)
    halves = [ones_where(lane_of(128) // 64 == j) for j in range(2)]
    swap = (lane // 64) % 2 if length == 64 else 0
    head_masks = [ones_where((lane % 64) // head_size == (swap ^ i)) for i in range(4)]
    low = lane_of(128) < 64
    attended = [[] for _ in range(4)]

    def scores_of(half, t):
        lanes = slice(half * 128, (half + 1) * 128)
        query_half = jnp.concatenate([query[:length, lanes], query[length:, lanes]], axis=1)
        key_half = jnp.concatenate([key[:length, lanes], key[length:, lanes]], axis=1)
        key_rows = jnp.concatenate([placed(key_half, j, halves) for j in range(4)], axis=0)
        spread = jnp.concatenate(
            [query_half * head_masks[t * per_tile + i] for i in range(per_tile)], axis=0
        )
        return dot_nt(key_rows, spread)

    def weights_of(line):
        if mask is not None:
            line = line + mask()
        top = jnp.max(line, axis=0, keepdims=True)
        line = jnp.exp2((line - top) * (math.log2(math.e) / math.sqrt(head_size)))
        return (line * (1.0 / jnp.sum(line, axis=0, keepdims=True))).astype(BF16)

    def gather(half, t, probs):
        if length == 64:
            values = value_t[half * 64 : (half + 1) * 64]
            lhs = jnp.concatenate([placed(values, j, halves) for j in range(4)], axis=0)
            out = dot_nn(lhs, jnp.concatenate(probs, axis=0))
            for i in range(4):
                at = slice((i // 2) * 128, (i // 2 + 1) * 128)
                for pair in range(2):
                    a = out[pair * 128 + i * 16 : pair * 128 + (i + 1) * 16, at]
                    b = out[pair * 128 + 64 + i * 16 : pair * 128 + 64 + (i + 1) * 16, at]
                    if i % 2:
                        attended[pair].append(pltpu.roll(jnp.where(low, b, a), 64, 1))
                    else:
                        attended[pair].append(jnp.where(low, a, b))
            return
        for pair in range(2):
            rows = slice(half * 64 + t * 32, half * 64 + (t + 1) * 32)
            values = value_t[rows, pair * 256 : (pair + 1) * 256]
            rest = jnp.zeros_like(values[:, :128])
            lhs = jnp.concatenate(
                [
                    jnp.concatenate([values[:, :128], rest], axis=1),
                    jnp.concatenate([rest, values[:, 128:]], axis=1),
                ],
                axis=0,
            )
            out = dot_nn(lhs, jnp.concatenate(probs[pair * 2 : pair * 2 + 2], axis=0))
            for j in range(2):
                for i in range(2):
                    attended[pair * 2 + j].append(
                        out[j * 32 + i * 16 : j * 32 + (i + 1) * 16, i * 128 : (i + 1) * 128]
                    )

    steps = [(half, t) for half in range(2) for t in range(4 // per_tile)]
    scores = scores_of(*steps[0])
    for k, step in enumerate(steps):
        yield
        ahead = scores_of(*steps[k + 1]) if k + 1 < len(steps) else None
        probs = []
        for j in range(4):
            probs.append(weights_of(scores[j * length : (j + 1) * length]))
            if length == 128:
                yield
        gather(*step, probs)
        yield
        scores = ahead
    yield
    if length == 64:
        new = []
        for pair in range(2):
            joined = jnp.concatenate(attended[pair], axis=0).astype(BF16)
            update = dot_tn(joined, weights.out)
            new += [lines[pair * 2] + update[:64], lines[pair * 2 + 1] + update[64:]]
        return new
    return [
        lines[j] + dot_tn(jnp.concatenate(attended[j], axis=0).astype(BF16), weights.out)
        for j in range(4)
    ]


def label_of(occ_ref, group, tile_y, tile_z):
    label = jnp.int32(0)
    for k in range(1, GROUP):
        label = label + k * occ_ref[tile_y, tile_z, group * GROUP + k]
    return label


def tile_labels(occ_ref, group):
    index = lax.broadcasted_iota(jnp.int32, (1, 1, occ_ref.shape[2]), 2)
    place = jnp.where(index // GROUP == group, index % GROUP, 0)
    return jnp.sum((occ_ref[...] * place).astype(F32), axis=-1, keepdims=True)


def same_tile_mask(labels, rows):
    made = []

    def mask():
        if not made:
            keys = jnp.concatenate([jnp.broadcast_to(label, (TILE, 128)) for label in labels], axis=0)
            one = jnp.where(keys == keys.T, 0.0, -BIG)[:rows]
            made.append(jnp.concatenate([one, one], axis=1))
        return made[0]

    return mask


def x_kernel(occ_ref, vol_ref, *refs):
    given, (out_ref, res_ref, starts_out) = refs[:5], refs[5:8]
    vin, whole, hs, done, starts, occ, sems, whole_sems, out_sems, table_sems = refs[8:18]
    weight_refs, weight_sems = refs[18:23], refs[23]
    chip, slab = lax.axis_index("chip"), lax.axis_index("slab")
    tile_y = chip // 2
    occ_load = pltpu.make_async_copy(occ_ref, occ, table_sems.at[1])
    occ_load.start()
    weight_loads = [
        pltpu.make_async_copy(given[0], weight_refs[0], weight_sems.at[0]),
        *[
            pltpu.make_async_copy(given[k].at[pl.ds(0, 1)], weight_refs[k], weight_sems.at[k])
            for k in range(1, 5)
        ],
    ]
    for copy in weight_loads:
        copy.start()
    occ_load.wait()
    tiles = []
    for g in range(4):
        start = (g * GROUP + label_of(occ, g, tile_y, slab)) * TILE
        starts[g : g + 1, :] = jnp.full((1, 128), start, jnp.int32)
        tiles.append(
            pltpu.make_async_copy(
                vol_ref.at[pl.ds(start, TILE)], vin.at[pl.ds(g * TILE, TILE)], sems.at[g]
            )
        )
    fetch = pltpu.make_async_copy(vol_ref, whole, whole_sems.at[0])
    store = pltpu.make_async_copy(whole, res_ref, whole_sems.at[1])
    for copy in tiles:
        copy.start()
    starts_copy = pltpu.make_async_copy(starts, starts_out, table_sems.at[0])
    starts_copy.start()
    for copy in weight_loads:
        copy.wait()
    weights = Weights(0, *weight_refs)
    for copy in tiles:
        copy.wait()
    fetch.start()
    outs = []
    held = hs.reshape(64, STRIDE, 128)
    places = [pl.ds(j, 64, stride=STRIDE) for j in range(32)]
    for half in range(2):
        rows = vin[:, :, half * 8 : (half + 1) * 8, :].astype(F32)
        held[:, :32, :] = rows.reshape(64, 32, 128)
        lines = [hs[at, :] for at in places]
        new = staggered([attend_quad(lines[4 * u : 4 * u + 4], weights) for u in range(8)])
        for at, line in zip(places, new):
            hs[at, :] = line
        done[half] = held[:, :32, :].astype(BF16)
        outs.append(pltpu.make_async_copy(done.at[half], out_ref.at[half], out_sems.at[half]))
        outs[-1].start()
        if half == 0:
            fetch.wait()
            store.start()
    for copy in [store, *outs, starts_copy]:
        copy.wait()


def y_kernel(occ_ref, in_ref, *refs):
    weight_refs, (keep_ref, send_ref, hs) = refs[:5], refs[5:]
    core = lax.axis_index("core")
    held = hs.reshape(4, 16, 2, 4, Y_STRIDE, 128)
    for side in range(2):
        held[:, :, side, :, :8, :] = in_ref[side].astype(F32).reshape(4, 16, 4, 8, 128)
    weights = Weights(1, *weight_refs)
    labels = tile_labels(occ_ref, lax.axis_index("slab"))
    masks = [same_tile_mask([labels[k, t : t + 1] for k in range(8)], 128) for t in range(4)]
    places = [
        pl.ds(k * 128 * Y_STRIDE + z, 128, stride=Y_STRIDE) for k in range(4) for z in range(8)
    ]
    lines = [hs[at, :] for at in places]
    new = staggered(
        [attend_quad(lines[4 * u : 4 * u + 4], weights, masks[u // 2]) for u in range(8)]
    )
    for at, line in zip(places, new):
        hs[at, :] = line
    for k in range(4):
        for p in range(32):
            for ref, side in ((keep_ref, core), (send_ref, 1 - core)):
                rows = [held[k, p // 2, p % 2, side * 2 + j, :8, :] for j in range(2)]
                ref[k, p] = jnp.concatenate(rows, axis=0).astype(BF16)


def z_kernel(occ_ref, kept_ref, got_ref, *refs):
    weight_refs, (out_ref,) = refs[:5], refs[5:]
    first = lax.axis_index("core") == 0
    weights = Weights(2, *weight_refs)

    labels = tile_labels(occ_ref, lax.axis_index("slab"))
    masks = [
        same_tile_mask([labels[k, t : t + 1] for t in range(4)] * 2, 64) for k in range(8)
    ]
    lines = []
    for u in range(32):
        pair = ([], [])
        for t in range(4):
            for ref in (kept_ref, got_ref):
                both = ref[t, u].astype(F32)
                pair[0].append(both[:8])
                pair[1].append(both[8:])
        lines += [jnp.concatenate(pair[0], axis=0), jnp.concatenate(pair[1], axis=0)]
    new = staggered(
        [attend_quad(lines[4 * u : 4 * u + 4], weights, masks[u // 2]) for u in range(16)]
    )
    for j in range(64):
        for t in range(4):
            kept, got = new[j][t * 16 : t * 16 + 8], new[j][t * 16 + 8 : t * 16 + 16]
            ordered = jnp.concatenate(
                [jnp.where(first, kept, got), jnp.where(first, got, kept)], axis=0
            )
            rows = slice((j % 2) * 16, (j % 2 + 1) * 16)
            u = j // 2
            out_ref[u % 2, t * 16 + u // 2, rows, :] = ordered.astype(BF16)


def merge_kernel(starts_ref, new_ref, res_in_ref, res_ref, sems):
    del res_in_ref
    starts = starts_ref[...]
    copies = []
    for g in range(4):
        start = pl.multiple_of(starts[g, 0], TILE)
        for side in range(2):
            copies.append(
                pltpu.make_async_copy(
                    new_ref.at[side, pl.ds(g * TILE, TILE)],
                    res_ref.at[pl.ds(start, TILE), pl.ds(side * 2, 2)],
                    sems.at[g * 2 + side],
                )
            )
            copies[-1].start()
    for copy in copies:
        copy.wait()


VMEM = pl.BlockSpec(memory_space=pltpu.VMEM)
ANY = pl.BlockSpec(memory_space=pl.ANY)
HBM = pl.BlockSpec(memory_space=pltpu.HBM)
PARAMS = pltpu.CompilerParams(vmem_limit_bytes=VMEM_BYTES)


def body(volume, occupancy, gains, w_query, w_key, w_value, w_out):
    params = (gains, w_query, w_key, w_value, w_out)
    occupancy = jnp.transpose(occupancy, (1, 2, 0))
    table = jax.ShapeDtypeStruct((8, 128), jnp.int32)
    after_x, copied, starts = pl.pallas_call(
        x_kernel,
        out_shape=(
            jax.ShapeDtypeStruct((2, 64, 32, 128), BF16),
            jax.ShapeDtypeStruct(volume.shape, BF16),
            table,
        ),
        in_specs=[HBM, HBM, *[HBM] * 5],
        out_specs=(HBM,) * 3,
        scratch_shapes=[
            pltpu.VMEM((64, 4, 16, 128), BF16),
            pltpu.VMEM(volume.shape, BF16),
            pltpu.VMEM((64 * STRIDE, 128), F32),
            pltpu.VMEM((2, 64, 32, 128), BF16),
            pltpu.VMEM(table.shape, table.dtype),
            pltpu.SMEM(occupancy.shape, jnp.int32),
            pltpu.SemaphoreType.DMA((4,)),
            pltpu.SemaphoreType.DMA((2,)),
            pltpu.SemaphoreType.DMA((2,)),
            pltpu.SemaphoreType.DMA((2,)),
            pltpu.VMEM(gains.shape, gains.dtype),
            *[pltpu.VMEM((1, *array.shape[1:]), array.dtype) for array in params[1:]],
            pltpu.SemaphoreType.DMA((5,)),
        ],
        compiler_params=pltpu.CompilerParams(vmem_limit_bytes=60 * 2**20),
        name="x_phase",
    )(occupancy, volume, *params)

    every = ("core", "slab", "chip")
    planes = lax.all_to_all(after_x.reshape(128, 32, 128), every, 0, 0, tiled=True)

    half = jax.ShapeDtypeStruct((4, 32, 16, 128), BF16)
    kept, sent = pl.pallas_call(
        y_kernel,
        out_shape=(half, half),
        in_specs=[VMEM] * 7,
        out_specs=(VMEM, VMEM),
        scratch_shapes=[pltpu.VMEM((4 * 128 * Y_STRIDE, 128), F32)],
        compiler_params=PARAMS,
        name="y_phase",
    )(occupancy, planes.reshape(2, 64, 32, 128), *params)

    got = lax.ppermute(sent, "core", [(0, 1), (1, 0)])

    after_z = pl.pallas_call(
        z_kernel,
        out_shape=jax.ShapeDtypeStruct((2, 64, 32, 128), BF16),
        in_specs=[VMEM] * 8,
        out_specs=VMEM,
        compiler_params=PARAMS,
        name="z_phase",
    )(occupancy, kept, got, *params)

    home = lax.all_to_all(after_z.reshape(128, 32, 128), every, 0, 0, tiled=True)

    return pl.pallas_call(
        merge_kernel,
        out_shape=jax.ShapeDtypeStruct(volume.shape, BF16),
        in_specs=[VMEM, ANY, HBM],
        out_specs=HBM,
        scratch_shapes=[pltpu.SemaphoreType.DMA((8,))],
        input_output_aliases={2: 0},
        compiler_params=PARAMS,
        name="merge",
    )(starts, home.reshape(2, 64, 2, 16, 128), copied)


def solution(mesh):
    devices = mesh.devices.reshape(mesh.shape["slab"], -1, 2)
    cores = jax.sharding.Mesh(devices, ("slab", "chip", "core"))
    volume = P(None, ("chip", "core"), "slab", None)
    placed = (volume, P(), P(), P(), P(), P(), P())
    return jax.shard_map(body, mesh=cores, in_specs=placed, out_specs=volume, check_vma=False)
```

```python
import functools
import math

import jax
import jax.numpy as jnp
from jax import lax
from jax.experimental import pallas as pl
from jax.experimental.pallas import tpu as pltpu
from jax.sharding import PartitionSpec as P

HEADS = 8
TILE = 16
GROUP = 4
BF16 = jnp.bfloat16
F32 = jnp.float32
BIG = 1e30
Y_STRIDE = 9
STRIDE = 36
GAP = 1
VMEM_BYTES = 48 * 2**20


def normalise(rows, gain):
    width = rows.shape[1]
    centred = rows - jnp.sum(rows, axis=-1, keepdims=True) * (1.0 / width)
    total = jnp.sum(centred * centred, axis=-1, keepdims=True)
    return (centred * lax.rsqrt(total + 1e-05 * width) * gain).astype(BF16)


def dot_nt(a, b):
    return lax.dot_general(a, b, (((1,), (1,)), ((), ())), preferred_element_type=F32)


def dot_tn(a, b):
    return lax.dot_general(a, b, (((0,), (0,)), ((), ())), preferred_element_type=F32)


def dot_nn(a, b):
    return jnp.dot(a, b, preferred_element_type=F32)


def lane_of(width):
    return lax.broadcasted_iota(jnp.int32, (1, width), 1)


def ones_where(condition):
    return jnp.where(condition, 1.0, 0.0).astype(BF16)


def paired(weight):
    low = lane_of(128) < 64
    wide = weight.astype(F32)
    lo, hi = jnp.where(low, wide, 0.0), jnp.where(low, 0.0, wide)
    first = jnp.concatenate([lo, pltpu.roll(hi, 64, 1)], axis=1)
    second = jnp.concatenate([pltpu.roll(lo, 64, 1), hi], axis=1)
    return jnp.concatenate([first, second], axis=0).astype(BF16)


def placed(block, j, low):
    tile = block[:, (j // 2) * 128 : (j // 2 + 1) * 128] * low[j % 2]
    rest = jnp.zeros_like(tile)
    return jnp.concatenate([tile, rest] if j < 2 else [rest, tile], axis=1)


class Weights:
    def __init__(self, phase, gain_ref, w_query_ref, w_key_ref, w_value_ref, w_out_ref):
        self.gain = gain_ref[phase : phase + 1, :] * math.sqrt(128)
        self.query = paired(w_query_ref[phase])
        self.key = paired(w_key_ref[phase])
        self.value_t = w_value_ref[phase].astype(F32).T.astype(BF16)
        self.out = w_out_ref[phase]


def staggered(quads, finish):
    active, turn, started = [], 0, 0
    while active or started < len(quads):
        if started < len(quads) and turn % GAP == 0:
            active.append(started)
            started += 1
        for which in list(active)[::-1]:
            try:
                next(quads[which])
            except StopIteration as stop:
                active.remove(which)
                finish(which, stop.value)
        turn += 1


def attend_quad(load, weights, mask=None):
    lines = load()
    length, width = lines[0].shape
    head_size = width // HEADS
    per_tile = 256 // length
    normed = normalise(jnp.concatenate(lines, axis=0), weights.gain)
    yield
    part = [normed[j * length : (j + 1) * length] for j in range(4)]
    beside = jnp.concatenate(
        [jnp.concatenate(part[0:2], axis=1), jnp.concatenate(part[2:4], axis=1)], axis=0
    )
    query = dot_nn(beside, weights.query).astype(BF16)
    key = dot_nn(beside, weights.key).astype(BF16)
    value_t = dot_nt(weights.value_t, normed).astype(BF16)
    yield
    lane = lane_of(256)
    halves = [ones_where(lane_of(128) // 64 == j) for j in range(2)]
    swap = (lane // 64) % 2 if length == 64 else 0
    head_masks = [ones_where((lane % 64) // head_size == (swap ^ i)) for i in range(4)]
    low = lane_of(128) < 64
    attended = [[] for _ in range(4)]

    def scores_of(half, t):
        lanes = slice(half * 128, (half + 1) * 128)
        query_half = jnp.concatenate([query[:length, lanes], query[length:, lanes]], axis=1)
        key_half = jnp.concatenate([key[:length, lanes], key[length:, lanes]], axis=1)
        key_rows = jnp.concatenate([placed(key_half, j, halves) for j in range(4)], axis=0)
        spread = jnp.concatenate(
            [query_half * head_masks[t * per_tile + i] for i in range(per_tile)], axis=0
        )
        return dot_nt(key_rows, spread)

    def weights_of(line):
        if mask is not None:
            line = line + mask()
        top = jnp.max(line, axis=0, keepdims=True)
        line = jnp.exp2((line - top) * (math.log2(math.e) / math.sqrt(head_size)))
        return (line * (1.0 / jnp.sum(line, axis=0, keepdims=True))).astype(BF16)

    def gather(half, t, probs):
        if length == 64:
            values = value_t[half * 64 : (half + 1) * 64]
            lhs = jnp.concatenate([placed(values, j, halves) for j in range(4)], axis=0)
            out = dot_nn(lhs, jnp.concatenate(probs, axis=0))
            for i in range(4):
                at = slice((i // 2) * 128, (i // 2 + 1) * 128)
                for pair in range(2):
                    a = out[pair * 128 + i * 16 : pair * 128 + (i + 1) * 16, at]
                    b = out[pair * 128 + 64 + i * 16 : pair * 128 + 64 + (i + 1) * 16, at]
                    if i % 2:
                        attended[pair].append(pltpu.roll(jnp.where(low, b, a), 64, 1))
                    else:
                        attended[pair].append(jnp.where(low, a, b))
            return
        for pair in range(2):
            rows = slice(half * 64 + t * 32, half * 64 + (t + 1) * 32)
            values = value_t[rows, pair * 256 : (pair + 1) * 256]
            rest = jnp.zeros_like(values[:, :128])
            lhs = jnp.concatenate(
                [
                    jnp.concatenate([values[:, :128], rest], axis=1),
                    jnp.concatenate([rest, values[:, 128:]], axis=1),
                ],
                axis=0,
            )
            out = dot_nn(lhs, jnp.concatenate(probs[pair * 2 : pair * 2 + 2], axis=0))
            for j in range(2):
                for i in range(2):
                    attended[pair * 2 + j].append(
                        out[j * 32 + i * 16 : j * 32 + (i + 1) * 16, i * 128 : (i + 1) * 128]
                    )

    steps = [(half, t) for half in range(2) for t in range(4 // per_tile)]
    scores = scores_of(*steps[0])
    for k, step in enumerate(steps):
        yield
        ahead = scores_of(*steps[k + 1]) if k + 1 < len(steps) else None
        probs = []
        for j in range(4):
            probs.append(weights_of(scores[j * length : (j + 1) * length]))
            if length == 128:
                yield
        gather(*step, probs)
        yield
        scores = ahead
    yield
    lines = load()
    if length == 64:
        new = []
        for pair in range(2):
            joined = jnp.concatenate(attended[pair], axis=0).astype(BF16)
            update = dot_tn(joined, weights.out)
            new += [lines[pair * 2] + update[:64], lines[pair * 2 + 1] + update[64:]]
        return new
    return [
        lines[j] + dot_tn(jnp.concatenate(attended[j], axis=0).astype(BF16), weights.out)
        for j in range(4)
    ]


def label_of(occ_ref, group, tile_y, tile_z):
    label = jnp.int32(0)
    for k in range(1, GROUP):
        label = label + k * occ_ref[tile_y, tile_z, group * GROUP + k]
    return label


def tile_marks(occ_ref, group):
    index = lax.broadcasted_iota(jnp.int32, (1, 1, occ_ref.shape[2]), 2)
    return jnp.where(index // GROUP == group, occ_ref[...], 0).astype(F32)


def same_tile_mask(mask_ref, marks):
    marks = jnp.concatenate([jnp.broadcast_to(m, (TILE, m.shape[1])) for m in marks], axis=0)
    marks = marks.astype(BF16)
    mask_ref[...] = (dot_nt(marks[: mask_ref.shape[0]], marks) - 1.0) * BIG
    return lambda: jnp.concatenate([mask_ref[...]] * 2, axis=1)


def x_kernel(occ_ref, vol_ref, *refs):
    given, (out_ref, res_ref, starts_out) = refs[:5], refs[5:8]
    vin, whole, hs, done, starts, occ, sems, whole_sems, out_sems, table_sems = refs[8:18]
    weight_refs, weight_sems = refs[18:23], refs[23]
    chip, slab = lax.axis_index("chip"), lax.axis_index("slab")
    tile_y = chip // 2
    occ_load = pltpu.make_async_copy(occ_ref, occ, table_sems.at[1])
    occ_load.start()
    weight_loads = [
        pltpu.make_async_copy(given[0], weight_refs[0], weight_sems.at[0]),
        *[
            pltpu.make_async_copy(given[k].at[pl.ds(0, 1)], weight_refs[k], weight_sems.at[k])
            for k in range(1, 5)
        ],
    ]
    for copy in weight_loads:
        copy.start()
    occ_load.wait()
    tiles = []
    for g in range(4):
        start = (g * GROUP + label_of(occ, g, tile_y, slab)) * TILE
        starts[g : g + 1, :] = jnp.full((1, 128), start, jnp.int32)
        tiles.append(
            pltpu.make_async_copy(
                vol_ref.at[pl.ds(start, TILE)], vin.at[pl.ds(g * TILE, TILE)], sems.at[g]
            )
        )
    fetch = pltpu.make_async_copy(vol_ref, whole, whole_sems.at[0])
    store = pltpu.make_async_copy(whole, res_ref, whole_sems.at[1])
    for copy in tiles:
        copy.start()
    starts_copy = pltpu.make_async_copy(starts, starts_out, table_sems.at[0])
    starts_copy.start()
    for copy in weight_loads:
        copy.wait()
    weights = Weights(0, *weight_refs)
    for copy in tiles:
        copy.wait()
    fetch.start()
    outs = []
    held = hs.reshape(2, 64, STRIDE, 128)

    def load_quad(u):
        half = u // 8
        asked = []

        def load():
            if u % 8 == 0 and not asked:
                rows = vin[:, :, half * 8 : (half + 1) * 8, :].astype(F32)
                held[half, :, :32, :] = rows.reshape(64, 32, 128)
            if u == 15 and not asked:
                fetch.wait()
                store.start()
            asked.append(u)
            return [hs[place(u, j), :] for j in range(4)]

        return load

    def place(u, j):
        return pl.ds((u // 8) * 64 * STRIDE + (u % 8) * 4 + j, 64, stride=STRIDE)

    def finish(u, new):
        for j in range(4):
            hs[place(u, j), :] = new[j]
        if u % 8 == 7:
            half = u // 8
            done[half] = held[half, :, :32, :].astype(BF16)
            outs.append(pltpu.make_async_copy(done.at[half], out_ref.at[half], out_sems.at[half]))
            outs[-1].start()

    staggered([attend_quad(load_quad(u), weights) for u in range(16)], finish)
    for copy in [store, *outs, starts_copy]:
        copy.wait()


def y_kernel(occ_ref, in_ref, *refs):
    weight_refs, (keep_ref, send_ref, hs, mask_ref) = refs[:5], refs[5:]
    core = lax.axis_index("core")
    held = hs.reshape(4, 16, 2, 4, Y_STRIDE, 128)
    for side in range(2):
        held[:, :, side, :, :8, :] = in_ref[side].astype(F32).reshape(4, 16, 4, 8, 128)
    weights = Weights(1, *weight_refs)
    marks = tile_marks(occ_ref, lax.axis_index("slab"))
    masks = [
        same_tile_mask(mask_ref.at[t], [marks[k, t : t + 1] for k in range(8)]) for t in range(4)
    ]

    def place(u, j):
        return pl.ds((u // 2) * 128 * Y_STRIDE + (u % 2) * 4 + j, 128, stride=Y_STRIDE)

    def load_quad(u):
        return lambda: [hs[place(u, j), :] for j in range(4)]

    def finish(u, new):
        for j in range(4):
            hs[place(u, j), :] = new[j]
        if u % 2:
            k = u // 2
            for p in range(32):
                for ref, side in ((keep_ref, core), (send_ref, 1 - core)):
                    rows = [held[k, p // 2, p % 2, side * 2 + j, :8, :] for j in range(2)]
                    ref[k, p] = jnp.concatenate(rows, axis=0).astype(BF16)

    staggered([attend_quad(load_quad(u), weights, masks[u // 2]) for u in range(8)], finish)


def z_kernel(occ_ref, kept_ref, got_ref, *refs):
    weight_refs, (out_ref, mask_ref) = refs[:5], refs[5:]
    first = lax.axis_index("core") == 0
    weights = Weights(2, *weight_refs)

    marks = tile_marks(occ_ref, lax.axis_index("slab"))
    masks = [
        same_tile_mask(mask_ref.at[k], [marks[k, t : t + 1] for t in range(4)] * 2)
        for k in range(8)
    ]

    def load_quad(quad):
        lines = []

        def load():
            if not lines:
                for u in (quad * 2, quad * 2 + 1):
                    pair = ([], [])
                    for t in range(4):
                        for ref in (kept_ref, got_ref):
                            both = ref[t, u].astype(F32)
                            pair[0].append(both[:8])
                            pair[1].append(both[8:])
                    lines.extend(jnp.concatenate(rows, axis=0) for rows in pair)
            return lines

        return load

    def finish(quad, new):
        for j in range(4):
            u = quad * 2 + j // 2
            for t in range(4):
                kept, got = new[j][t * 16 : t * 16 + 8], new[j][t * 16 + 8 : t * 16 + 16]
                ordered = jnp.concatenate(
                    [jnp.where(first, kept, got), jnp.where(first, got, kept)], axis=0
                )
                rows = slice((j % 2) * 16, (j % 2 + 1) * 16)
                out_ref[u % 2, t * 16 + u // 2, rows, :] = ordered.astype(BF16)

    staggered([attend_quad(load_quad(u), weights, masks[u // 2]) for u in range(16)], finish)


def merge_kernel(starts_ref, new_ref, res_in_ref, res_ref, sems):
    del res_in_ref
    starts = starts_ref[...]
    copies = []
    for g in range(4):
        start = pl.multiple_of(starts[g, 0], TILE)
        for side in range(2):
            copies.append(
                pltpu.make_async_copy(
                    new_ref.at[side, pl.ds(g * TILE, TILE)],
                    res_ref.at[pl.ds(start, TILE), pl.ds(side * 2, 2)],
                    sems.at[g * 2 + side],
                )
            )
            copies[-1].start()
    for copy in copies:
        copy.wait()


VMEM = pl.BlockSpec(memory_space=pltpu.VMEM)
ANY = pl.BlockSpec(memory_space=pl.ANY)
HBM = pl.BlockSpec(memory_space=pltpu.HBM)
PARAMS = pltpu.CompilerParams(vmem_limit_bytes=VMEM_BYTES)


def body(volume, occupancy, gains, w_query, w_key, w_value, w_out):
    params = (gains, w_query, w_key, w_value, w_out)
    occupancy = jnp.transpose(occupancy, (1, 2, 0))
    table = jax.ShapeDtypeStruct((8, 128), jnp.int32)
    after_x, copied, starts = pl.pallas_call(
        x_kernel,
        out_shape=(
            jax.ShapeDtypeStruct((2, 64, 32, 128), BF16),
            jax.ShapeDtypeStruct(volume.shape, BF16),
            table,
        ),
        in_specs=[HBM, HBM, *[HBM] * 5],
        out_specs=(HBM,) * 3,
        scratch_shapes=[
            pltpu.VMEM((64, 4, 16, 128), BF16),
            pltpu.VMEM(volume.shape, BF16),
            pltpu.VMEM((2 * 64 * STRIDE, 128), F32),
            pltpu.VMEM((2, 64, 32, 128), BF16),
            pltpu.VMEM(table.shape, table.dtype),
            pltpu.SMEM(occupancy.shape, jnp.int32),
            pltpu.SemaphoreType.DMA((4,)),
            pltpu.SemaphoreType.DMA((2,)),
            pltpu.SemaphoreType.DMA((2,)),
            pltpu.SemaphoreType.DMA((2,)),
            pltpu.VMEM(gains.shape, gains.dtype),
            *[pltpu.VMEM((1, *array.shape[1:]), array.dtype) for array in params[1:]],
            pltpu.SemaphoreType.DMA((5,)),
        ],
        compiler_params=pltpu.CompilerParams(vmem_limit_bytes=60 * 2**20),
        name="x_phase",
    )(occupancy, volume, *params)

    every = ("core", "slab", "chip")
    planes = lax.all_to_all(after_x.reshape(128, 32, 128), every, 0, 0, tiled=True)

    half = jax.ShapeDtypeStruct((4, 32, 16, 128), BF16)
    kept, sent = pl.pallas_call(
        y_kernel,
        out_shape=(half, half),
        in_specs=[VMEM] * 7,
        out_specs=(VMEM, VMEM),
        scratch_shapes=[
            pltpu.VMEM((4 * 128 * Y_STRIDE, 128), F32),
            pltpu.VMEM((4, 128, 128), F32),
        ],
        compiler_params=PARAMS,
        name="y_phase",
    )(occupancy, planes.reshape(2, 64, 32, 128), *params)

    got = lax.ppermute(sent, "core", [(0, 1), (1, 0)])

    after_z = pl.pallas_call(
        z_kernel,
        out_shape=jax.ShapeDtypeStruct((2, 64, 32, 128), BF16),
        in_specs=[VMEM] * 8,
        out_specs=VMEM,
        scratch_shapes=[pltpu.VMEM((8, 64, 128), F32)],
        compiler_params=PARAMS,
        name="z_phase",
    )(occupancy, kept, got, *params)

    home = lax.all_to_all(after_z.reshape(128, 32, 128), every, 0, 0, tiled=True)

    return pl.pallas_call(
        merge_kernel,
        out_shape=jax.ShapeDtypeStruct(volume.shape, BF16),
        in_specs=[VMEM, ANY, HBM],
        out_specs=HBM,
        scratch_shapes=[pltpu.SemaphoreType.DMA((8,))],
        input_output_aliases={2: 0},
        compiler_params=PARAMS,
        name="merge",
    )(starts, home.reshape(2, 64, 2, 16, 128), copied)


def solution(mesh):
    devices = mesh.devices.reshape(mesh.shape["slab"], -1, 2)
    cores = jax.sharding.Mesh(devices, ("slab", "chip", "core"))
    volume = P(None, ("chip", "core"), "slab", None)
    placed = (volume, P(), P(), P(), P(), P(), P())
    return jax.shard_map(body, mesh=cores, in_specs=placed, out_specs=volume, check_vma=False)
```

```python
import functools
import math

import jax
import jax.numpy as jnp
from jax import lax
from jax.experimental import pallas as pl
from jax.experimental.pallas import tpu as pltpu
from jax.sharding import PartitionSpec as P

HEADS = 8
TILE = 16
GROUP = 4
BF16 = jnp.bfloat16
F32 = jnp.float32
BIG = 1e30
Y_STRIDE = 9
STRIDE = 36
GAP = 1
VMEM_BYTES = 48 * 2**20


def normalise(rows, gain):
    width = rows.shape[1]
    centred = rows - jnp.sum(rows, axis=-1, keepdims=True) * (1.0 / width)
    total = jnp.sum(centred * centred, axis=-1, keepdims=True)
    return (centred * lax.rsqrt(total + 1e-05 * width) * gain).astype(BF16)


def dot_nt(a, b):
    return lax.dot_general(a, b, (((1,), (1,)), ((), ())), preferred_element_type=F32)


def dot_tn(a, b):
    return lax.dot_general(a, b, (((0,), (0,)), ((), ())), preferred_element_type=F32)


def dot_nn(a, b):
    return jnp.dot(a, b, preferred_element_type=F32)


def lane_of(width):
    return lax.broadcasted_iota(jnp.int32, (1, width), 1)


def ones_where(condition):
    return jnp.where(condition, 1.0, 0.0).astype(BF16)


def paired(weight):
    low = lane_of(128) < 64
    wide = weight.astype(F32)
    lo, hi = jnp.where(low, wide, 0.0), jnp.where(low, 0.0, wide)
    first = jnp.concatenate([lo, pltpu.roll(hi, 64, 1)], axis=1)
    second = jnp.concatenate([pltpu.roll(lo, 64, 1), hi], axis=1)
    return jnp.concatenate([first, second], axis=0).astype(BF16)


def placed(block, j, low):
    tile = block[:, (j // 2) * 128 : (j // 2 + 1) * 128] * low[j % 2]
    rest = jnp.zeros_like(tile)
    return jnp.concatenate([tile, rest] if j < 2 else [rest, tile], axis=1)


class Weights:
    def __init__(self, phase, gain_ref, w_query_ref, w_key_ref, w_value_ref, w_out_ref):
        self.gain = gain_ref[phase : phase + 1, :] * math.sqrt(128)
        self.query = paired(w_query_ref[phase])
        self.key = paired(w_key_ref[phase])
        self.value_t = w_value_ref[phase].astype(F32).T.astype(BF16)
        self.out = w_out_ref[phase]


def staggered(quads, finish):
    active, turn, started = [], 0, 0
    while active or started < len(quads):
        if started < len(quads) and turn % GAP == 0:
            active.append(started)
            started += 1
        for which in list(active)[::-1]:
            try:
                next(quads[which])
            except StopIteration as stop:
                active.remove(which)
                finish(which, stop.value)
        turn += 1


class SpareLanes:
    def __init__(self, marks):
        marks = jnp.concatenate([jnp.broadcast_to(m, (TILE, m.shape[1])) for m in marks], axis=0)
        marks = marks.astype(BF16)
        lane = lane_of(128)
        row = lax.broadcasted_iota(jnp.int32, (marks.shape[1], 1), 0)
        self.keys, self.queries = [], []
        for t in range(2):
            at = (lane % 64) - 32 * (1 - t)
            wide = dot_nn(marks, ones_where(at == row))
            inside = jnp.logical_and(at >= 0, at < marks.shape[1])
            other = (wide - jnp.where(inside, 1.0, 0.0)) * BIG
            self.queries.append(jnp.concatenate([other, other], axis=1).astype(BF16))
            self.keys.append([jnp.where(lane // 64 == j, wide, 0.0).astype(BF16) for j in range(2)])

    def spread(self, query, t, lanes):
        return jnp.where(lanes, query, self.queries[t])

    def place(self, key, t, j):
        lane = lane_of(128)
        own = jnp.logical_and(lane // 64 == j % 2, (lane % 64) // 32 == t)
        tile = jnp.where(own, key[:, (j // 2) * 128 : (j // 2 + 1) * 128], self.keys[t][j % 2])
        rest = jnp.zeros_like(tile)
        return jnp.concatenate([tile, rest] if j < 2 else [rest, tile], axis=1)


def attend_quad(load, weights, mask=None):
    lines = load()
    length, width = lines[0].shape
    head_size = width // HEADS
    per_tile = 256 // length
    normed = normalise(jnp.concatenate(lines, axis=0), weights.gain)
    yield
    part = [normed[j * length : (j + 1) * length] for j in range(4)]
    beside = jnp.concatenate(
        [jnp.concatenate(part[0:2], axis=1), jnp.concatenate(part[2:4], axis=1)], axis=0
    )
    query = dot_nn(beside, weights.query).astype(BF16)
    key = dot_nn(beside, weights.key).astype(BF16)
    value_t = dot_nt(weights.value_t, normed).astype(BF16)
    yield
    lane = lane_of(256)
    halves = [ones_where(lane_of(128) // 64 == j) for j in range(2)]
    swap = (lane // 64) % 2 if length == 64 else 0
    head_masks = [ones_where((lane % 64) // head_size == (swap ^ i)) for i in range(4)]
    low = lane_of(128) < 64
    attended = [[] for _ in range(4)]

    def scores_of(half, t):
        lanes = slice(half * 128, (half + 1) * 128)
        query_half = jnp.concatenate([query[:length, lanes], query[length:, lanes]], axis=1)
        key_half = jnp.concatenate([key[:length, lanes], key[length:, lanes]], axis=1)
        if length == 128:
            key_rows = jnp.concatenate([mask.place(key_half, t, j) for j in range(4)], axis=0)
            heads = [(lane % 64) // head_size == t * per_tile + i for i in range(per_tile)]
            spread = jnp.concatenate([mask.spread(query_half, t, h) for h in heads], axis=0)
            return dot_nt(key_rows, spread)
        key_rows = jnp.concatenate([placed(key_half, j, halves) for j in range(4)], axis=0)
        spread = jnp.concatenate(
            [query_half * head_masks[t * per_tile + i] for i in range(per_tile)], axis=0
        )
        return dot_nt(key_rows, spread)

    def weights_of(line):
        if mask is not None and length == 64:
            line = line + mask()
        top = jnp.max(line, axis=0, keepdims=True)
        line = jnp.exp2((line - top) * (math.log2(math.e) / math.sqrt(head_size)))
        return (line * (1.0 / jnp.sum(line, axis=0, keepdims=True))).astype(BF16)

    def gather(half, t, probs):
        if length == 64:
            values = value_t[half * 64 : (half + 1) * 64]
            lhs = jnp.concatenate([placed(values, j, halves) for j in range(4)], axis=0)
            out = dot_nn(lhs, jnp.concatenate(probs, axis=0))
            for i in range(4):
                at = slice((i // 2) * 128, (i // 2 + 1) * 128)
                for pair in range(2):
                    a = out[pair * 128 + i * 16 : pair * 128 + (i + 1) * 16, at]
                    b = out[pair * 128 + 64 + i * 16 : pair * 128 + 64 + (i + 1) * 16, at]
                    if i % 2:
                        attended[pair].append(pltpu.roll(jnp.where(low, b, a), 64, 1))
                    else:
                        attended[pair].append(jnp.where(low, a, b))
            return
        for pair in range(2):
            rows = slice(half * 64 + t * 32, half * 64 + (t + 1) * 32)
            values = value_t[rows, pair * 256 : (pair + 1) * 256]
            rest = jnp.zeros_like(values[:, :128])
            lhs = jnp.concatenate(
                [
                    jnp.concatenate([values[:, :128], rest], axis=1),
                    jnp.concatenate([rest, values[:, 128:]], axis=1),
                ],
                axis=0,
            )
            out = dot_nn(lhs, jnp.concatenate(probs[pair * 2 : pair * 2 + 2], axis=0))
            for j in range(2):
                for i in range(2):
                    attended[pair * 2 + j].append(
                        out[j * 32 + i * 16 : j * 32 + (i + 1) * 16, i * 128 : (i + 1) * 128]
                    )

    steps = [(half, t) for half in range(2) for t in range(4 // per_tile)]
    scores = scores_of(*steps[0])
    for k, step in enumerate(steps):
        yield
        ahead = scores_of(*steps[k + 1]) if k + 1 < len(steps) else None
        probs = []
        for j in range(4):
            probs.append(weights_of(scores[j * length : (j + 1) * length]))
            if length == 128:
                yield
        gather(*step, probs)
        yield
        scores = ahead
    yield
    lines = load()
    if length == 64:
        new = []
        for pair in range(2):
            joined = jnp.concatenate(attended[pair], axis=0).astype(BF16)
            update = dot_tn(joined, weights.out)
            new += [lines[pair * 2] + update[:64], lines[pair * 2 + 1] + update[64:]]
        return new
    return [
        lines[j] + dot_tn(jnp.concatenate(attended[j], axis=0).astype(BF16), weights.out)
        for j in range(4)
    ]


def label_of(occ_ref, group, tile_y, tile_z):
    label = jnp.int32(0)
    for k in range(1, GROUP):
        label = label + k * occ_ref[tile_y, tile_z, group * GROUP + k]
    return label


def tile_marks(occ_ref, group):
    index = lax.broadcasted_iota(jnp.int32, (1, 1, occ_ref.shape[2]), 2)
    return jnp.where(index // GROUP == group, occ_ref[...], 0).astype(F32)


def same_tile_mask(mask_ref, marks):
    marks = jnp.concatenate([jnp.broadcast_to(m, (TILE, m.shape[1])) for m in marks], axis=0)
    marks = marks.astype(BF16)
    mask_ref[...] = (dot_nt(marks[: mask_ref.shape[0]], marks) - 1.0) * BIG
    return lambda: jnp.concatenate([mask_ref[...]] * 2, axis=1)


def x_kernel(occ_ref, vol_ref, *refs):
    given, (out_ref, res_ref, starts_out) = refs[:5], refs[5:8]
    vin, whole, hs, done, starts, occ, sems, whole_sems, out_sems, table_sems = refs[8:18]
    weight_refs, weight_sems = refs[18:23], refs[23]
    chip, slab = lax.axis_index("chip"), lax.axis_index("slab")
    tile_y = chip // 2
    occ_load = pltpu.make_async_copy(occ_ref, occ, table_sems.at[1])
    occ_load.start()
    weight_loads = [
        pltpu.make_async_copy(given[0], weight_refs[0], weight_sems.at[0]),
        *[
            pltpu.make_async_copy(given[k].at[pl.ds(0, 1)], weight_refs[k], weight_sems.at[k])
            for k in range(1, 5)
        ],
    ]
    for copy in weight_loads:
        copy.start()
    occ_load.wait()
    tiles = []
    for g in range(4):
        start = (g * GROUP + label_of(occ, g, tile_y, slab)) * TILE
        starts[g : g + 1, :] = jnp.full((1, 128), start, jnp.int32)
        tiles.append(
            pltpu.make_async_copy(
                vol_ref.at[pl.ds(start, TILE)], vin.at[pl.ds(g * TILE, TILE)], sems.at[g]
            )
        )
    fetch = pltpu.make_async_copy(vol_ref, whole, whole_sems.at[0])
    store = pltpu.make_async_copy(whole, res_ref, whole_sems.at[1])
    for copy in tiles:
        copy.start()
    starts_copy = pltpu.make_async_copy(starts, starts_out, table_sems.at[0])
    starts_copy.start()
    for copy in weight_loads:
        copy.wait()
    weights = Weights(0, *weight_refs)
    for copy in tiles:
        copy.wait()
    fetch.start()
    outs = []
    held = hs.reshape(2, 64, STRIDE, 128)

    def load_quad(u):
        half = u // 8
        asked = []

        def load():
            if u % 8 == 0 and not asked:
                rows = vin[:, :, half * 8 : (half + 1) * 8, :].astype(F32)
                held[half, :, :32, :] = rows.reshape(64, 32, 128)
            if u == 15 and not asked:
                fetch.wait()
                store.start()
            asked.append(u)
            return [hs[place(u, j), :] for j in range(4)]

        return load

    def place(u, j):
        return pl.ds((u // 8) * 64 * STRIDE + (u % 8) * 4 + j, 64, stride=STRIDE)

    def finish(u, new):
        for j in range(4):
            hs[place(u, j), :] = new[j]
        if u % 8 == 7:
            half = u // 8
            done[half] = held[half, :, :32, :].astype(BF16)
            outs.append(pltpu.make_async_copy(done.at[half], out_ref.at[half], out_sems.at[half]))
            outs[-1].start()

    staggered([attend_quad(load_quad(u), weights) for u in range(16)], finish)
    for copy in [store, *outs, starts_copy]:
        copy.wait()


def y_kernel(occ_ref, in_ref, *refs):
    weight_refs, (keep_ref, send_ref, hs) = refs[:5], refs[5:]
    core = lax.axis_index("core")
    held = hs.reshape(4, 16, 2, 4, Y_STRIDE, 128)
    for side in range(2):
        held[:, :, side, :, :8, :] = in_ref[side].astype(F32).reshape(4, 16, 4, 8, 128)
    weights = Weights(1, *weight_refs)
    marks = tile_marks(occ_ref, lax.axis_index("slab"))
    masks = [SpareLanes([marks[k, t : t + 1] for k in range(8)]) for t in range(4)]

    def place(u, j):
        return pl.ds((u // 2) * 128 * Y_STRIDE + (u % 2) * 4 + j, 128, stride=Y_STRIDE)

    def load_quad(u):
        return lambda: [hs[place(u, j), :] for j in range(4)]

    def finish(u, new):
        for j in range(4):
            hs[place(u, j), :] = new[j]
        if u % 2:
            k = u // 2
            for p in range(32):
                for ref, side in ((keep_ref, core), (send_ref, 1 - core)):
                    rows = [held[k, p // 2, p % 2, side * 2 + j, :8, :] for j in range(2)]
                    ref[k, p] = jnp.concatenate(rows, axis=0).astype(BF16)

    staggered([attend_quad(load_quad(u), weights, masks[u // 2]) for u in range(8)], finish)


def z_kernel(occ_ref, kept_ref, got_ref, *refs):
    weight_refs, (out_ref, mask_ref) = refs[:5], refs[5:]
    first = lax.axis_index("core") == 0
    weights = Weights(2, *weight_refs)

    marks = tile_marks(occ_ref, lax.axis_index("slab"))
    masks = [
        same_tile_mask(mask_ref.at[k], [marks[k, t : t + 1] for t in range(4)] * 2)
        for k in range(8)
    ]

    def load_quad(quad):
        lines = []

        def load():
            if not lines:
                for u in (quad * 2, quad * 2 + 1):
                    pair = ([], [])
                    for t in range(4):
                        for ref in (kept_ref, got_ref):
                            both = ref[t, u].astype(F32)
                            pair[0].append(both[:8])
                            pair[1].append(both[8:])
                    lines.extend(jnp.concatenate(rows, axis=0) for rows in pair)
            return lines

        return load

    def finish(quad, new):
        for j in range(4):
            u = quad * 2 + j // 2
            for t in range(4):
                kept, got = new[j][t * 16 : t * 16 + 8], new[j][t * 16 + 8 : t * 16 + 16]
                ordered = jnp.concatenate(
                    [jnp.where(first, kept, got), jnp.where(first, got, kept)], axis=0
                )
                rows = slice((j % 2) * 16, (j % 2 + 1) * 16)
                out_ref[u % 2, t * 16 + u // 2, rows, :] = ordered.astype(BF16)

    staggered([attend_quad(load_quad(u), weights, masks[u // 2]) for u in range(16)], finish)


def merge_kernel(starts_ref, new_ref, res_in_ref, res_ref, sems):
    del res_in_ref
    starts = starts_ref[...]
    copies = []
    for g in range(4):
        start = pl.multiple_of(starts[g, 0], TILE)
        for side in range(2):
            copies.append(
                pltpu.make_async_copy(
                    new_ref.at[side, pl.ds(g * TILE, TILE)],
                    res_ref.at[pl.ds(start, TILE), pl.ds(side * 2, 2)],
                    sems.at[g * 2 + side],
                )
            )
            copies[-1].start()
    for copy in copies:
        copy.wait()


VMEM = pl.BlockSpec(memory_space=pltpu.VMEM)
ANY = pl.BlockSpec(memory_space=pl.ANY)
HBM = pl.BlockSpec(memory_space=pltpu.HBM)
PARAMS = pltpu.CompilerParams(vmem_limit_bytes=VMEM_BYTES)


def body(volume, occupancy, gains, w_query, w_key, w_value, w_out):
    params = (gains, w_query, w_key, w_value, w_out)
    occupancy = jnp.transpose(occupancy, (1, 2, 0))
    table = jax.ShapeDtypeStruct((8, 128), jnp.int32)
    after_x, copied, starts = pl.pallas_call(
        x_kernel,
        out_shape=(
            jax.ShapeDtypeStruct((2, 64, 32, 128), BF16),
            jax.ShapeDtypeStruct(volume.shape, BF16),
            table,
        ),
        in_specs=[HBM, HBM, *[HBM] * 5],
        out_specs=(HBM,) * 3,
        scratch_shapes=[
            pltpu.VMEM((64, 4, 16, 128), BF16),
            pltpu.VMEM(volume.shape, BF16),
            pltpu.VMEM((2 * 64 * STRIDE, 128), F32),
            pltpu.VMEM((2, 64, 32, 128), BF16),
            pltpu.VMEM(table.shape, table.dtype),
            pltpu.SMEM(occupancy.shape, jnp.int32),
            pltpu.SemaphoreType.DMA((4,)),
            pltpu.SemaphoreType.DMA((2,)),
            pltpu.SemaphoreType.DMA((2,)),
            pltpu.SemaphoreType.DMA((2,)),
            pltpu.VMEM(gains.shape, gains.dtype),
            *[pltpu.VMEM((1, *array.shape[1:]), array.dtype) for array in params[1:]],
            pltpu.SemaphoreType.DMA((5,)),
        ],
        compiler_params=pltpu.CompilerParams(vmem_limit_bytes=60 * 2**20),
        name="x_phase",
    )(occupancy, volume, *params)

    every = ("core", "slab", "chip")
    planes = lax.all_to_all(after_x.reshape(128, 32, 128), every, 0, 0, tiled=True)

    half = jax.ShapeDtypeStruct((4, 32, 16, 128), BF16)
    kept, sent = pl.pallas_call(
        y_kernel,
        out_shape=(half, half),
        in_specs=[VMEM] * 7,
        out_specs=(VMEM, VMEM),
        scratch_shapes=[pltpu.VMEM((4 * 128 * Y_STRIDE, 128), F32)],
        compiler_params=PARAMS,
        name="y_phase",
    )(occupancy, planes.reshape(2, 64, 32, 128), *params)

    got = lax.ppermute(sent, "core", [(0, 1), (1, 0)])

    after_z = pl.pallas_call(
        z_kernel,
        out_shape=jax.ShapeDtypeStruct((2, 64, 32, 128), BF16),
        in_specs=[VMEM] * 8,
        out_specs=VMEM,
        scratch_shapes=[pltpu.VMEM((8, 64, 128), F32)],
        compiler_params=PARAMS,
        name="z_phase",
    )(occupancy, kept, got, *params)

    home = lax.all_to_all(after_z.reshape(128, 32, 128), every, 0, 0, tiled=True)

    return pl.pallas_call(
        merge_kernel,
        out_shape=jax.ShapeDtypeStruct(volume.shape, BF16),
        in_specs=[VMEM, ANY, HBM],
        out_specs=HBM,
        scratch_shapes=[pltpu.SemaphoreType.DMA((8,))],
        input_output_aliases={2: 0},
        compiler_params=PARAMS,
        name="merge",
    )(starts, home.reshape(2, 64, 2, 16, 128), copied)


def solution(mesh):
    devices = mesh.devices.reshape(mesh.shape["slab"], -1, 2)
    cores = jax.sharding.Mesh(devices, ("slab", "chip", "core"))
    volume = P(None, ("chip", "core"), "slab", None)
    placed = (volume, P(), P(), P(), P(), P(), P())
    return jax.shard_map(body, mesh=cores, in_specs=placed, out_specs=volume, check_vma=False)
```

```python
import functools
import math

import jax
import jax.numpy as jnp
from jax import lax
from jax.experimental import pallas as pl
from jax.experimental.pallas import tpu as pltpu
from jax.sharding import PartitionSpec as P

HEADS = 8
TILE = 16
GROUP = 4
BF16 = jnp.bfloat16
F32 = jnp.float32
BIG = 1e30
Y_STRIDE = 9
STRIDE = 36
GAP = 1
VMEM_BYTES = 48 * 2**20


def normalise(rows, gain):
    width = rows.shape[1]
    centred = rows - jnp.sum(rows, axis=-1, keepdims=True) * (1.0 / width)
    total = jnp.sum(centred * centred, axis=-1, keepdims=True)
    return (centred * lax.rsqrt(total + 1e-05 * width) * gain).astype(BF16)


def dot_nt(a, b):
    return lax.dot_general(a, b, (((1,), (1,)), ((), ())), preferred_element_type=F32)


def dot_tn(a, b):
    return lax.dot_general(a, b, (((0,), (0,)), ((), ())), preferred_element_type=F32)


def dot_nn(a, b):
    return jnp.dot(a, b, preferred_element_type=F32)


def lane_of(width):
    return lax.broadcasted_iota(jnp.int32, (1, width), 1)


def ones_where(condition):
    return jnp.where(condition, 1.0, 0.0).astype(BF16)


def paired(weight):
    low = lane_of(128) < 64
    wide = weight.astype(F32)
    lo, hi = jnp.where(low, wide, 0.0), jnp.where(low, 0.0, wide)
    first = jnp.concatenate([lo, pltpu.roll(hi, 64, 1)], axis=1)
    second = jnp.concatenate([pltpu.roll(lo, 64, 1), hi], axis=1)
    return jnp.concatenate([first, second], axis=0).astype(BF16)


def placed(block, j, low):
    tile = block[:, (j // 2) * 128 : (j // 2 + 1) * 128] * low[j % 2]
    rest = jnp.zeros_like(tile)
    return jnp.concatenate([tile, rest] if j < 2 else [rest, tile], axis=1)


class Weights:
    def __init__(self, phase, gain_ref, w_query_ref, w_key_ref, w_value_ref, w_out_ref):
        self.gain = gain_ref[phase : phase + 1, :] * math.sqrt(128)
        self.query = paired(w_query_ref[phase])
        self.key = paired(w_key_ref[phase])
        self.value_t = w_value_ref[phase].astype(F32).T.astype(BF16)
        self.out = w_out_ref[phase]


def staggered(quads, finish):
    active, turn, started = [], 0, 0
    while active or started < len(quads):
        if started < len(quads) and turn % GAP == 0:
            active.append(started)
            started += 1
        for which in list(active)[::-1]:
            try:
                next(quads[which])
            except StopIteration as stop:
                active.remove(which)
                finish(which, stop.value)
        turn += 1


class SpareLanes:
    def __init__(self, marks):
        marks = jnp.concatenate([jnp.broadcast_to(m, (TILE, m.shape[1])) for m in marks], axis=0)
        marks = marks.astype(BF16)
        lane = lane_of(128)
        row = lax.broadcasted_iota(jnp.int32, (marks.shape[1], 1), 0)
        self.keys, self.queries = [], []
        for t in range(2):
            at = (lane % 64) - 32 * (1 - t)
            wide = dot_nn(marks, ones_where(at == row))
            inside = jnp.logical_and(at >= 0, at < marks.shape[1])
            other = (wide - jnp.where(inside, 1.0, 0.0)) * BIG
            self.queries.append(jnp.concatenate([other, other], axis=1).astype(BF16))
            self.keys.append([jnp.where(lane // 64 == j, wide, 0.0).astype(BF16) for j in range(2)])

    def spread(self, query, t, lanes):
        return jnp.where(lanes, query, self.queries[t])

    def place(self, key, t, j):
        lane = lane_of(128)
        own = jnp.logical_and(lane // 64 == j % 2, (lane % 64) // 32 == t)
        tile = jnp.where(own, key[:, (j // 2) * 128 : (j // 2 + 1) * 128], self.keys[t][j % 2])
        rest = jnp.zeros_like(tile)
        return jnp.concatenate([tile, rest] if j < 2 else [rest, tile], axis=1)


def attend_quad(load, weights, mask=None):
    lines = load()
    length, width = lines[0].shape
    head_size = width // HEADS
    per_tile = 256 // length
    normed = normalise(jnp.concatenate(lines, axis=0), weights.gain)
    yield
    part = [normed[j * length : (j + 1) * length] for j in range(4)]
    beside = jnp.concatenate(
        [jnp.concatenate(part[0:2], axis=1), jnp.concatenate(part[2:4], axis=1)], axis=0
    )
    query = dot_nn(beside, weights.query).astype(BF16)
    key = dot_nn(beside, weights.key).astype(BF16)
    value_t = dot_nt(weights.value_t, normed).astype(BF16)
    yield
    lane = lane_of(256)
    halves = [ones_where(lane_of(128) // 64 == j) for j in range(2)]
    swap = (lane // 64) % 2 if length == 64 else 0
    head_masks = [ones_where((lane % 64) // head_size == (swap ^ i)) for i in range(4)]
    low = lane_of(128) < 64
    attended = [[] for _ in range(4)]

    def scores_of(half, t):
        lanes = slice(half * 128, (half + 1) * 128)
        query_half = jnp.concatenate([query[:length, lanes], query[length:, lanes]], axis=1)
        key_half = jnp.concatenate([key[:length, lanes], key[length:, lanes]], axis=1)
        if length == 128:
            key_rows = jnp.concatenate([mask.place(key_half, t, j) for j in range(4)], axis=0)
            heads = [(lane % 64) // head_size == t * per_tile + i for i in range(per_tile)]
            spread = jnp.concatenate([mask.spread(query_half, t, h) for h in heads], axis=0)
            return dot_nt(key_rows, spread)
        key_rows = jnp.concatenate([placed(key_half, j, halves) for j in range(4)], axis=0)
        spread = jnp.concatenate(
            [query_half * head_masks[t * per_tile + i] for i in range(per_tile)], axis=0
        )
        return dot_nt(key_rows, spread)

    def weights_of(line):
        if mask is not None and length == 64:
            line = line + mask()
        top = jnp.max(line, axis=0, keepdims=True)
        line = jnp.exp2((line - top) * (math.log2(math.e) / math.sqrt(head_size)))
        return (line * (1.0 / jnp.sum(line, axis=0, keepdims=True))).astype(BF16)

    def gather(half, t, probs):
        if length == 64:
            values = value_t[half * 64 : (half + 1) * 64]
            lhs = jnp.concatenate([placed(values, j, halves) for j in range(4)], axis=0)
            out = dot_nn(lhs, jnp.concatenate(probs, axis=0))
            for i in range(4):
                at = slice((i // 2) * 128, (i // 2 + 1) * 128)
                for pair in range(2):
                    a = out[pair * 128 + i * 16 : pair * 128 + (i + 1) * 16, at]
                    b = out[pair * 128 + 64 + i * 16 : pair * 128 + 64 + (i + 1) * 16, at]
                    if i % 2:
                        attended[pair].append(pltpu.roll(jnp.where(low, b, a), 64, 1))
                    else:
                        attended[pair].append(jnp.where(low, a, b))
            return
        for pair in range(2):
            rows = slice(half * 64 + t * 32, half * 64 + (t + 1) * 32)
            values = value_t[rows, pair * 256 : (pair + 1) * 256]
            rest = jnp.zeros_like(values[:, :128])
            lhs = jnp.concatenate(
                [
                    jnp.concatenate([values[:, :128], rest], axis=1),
                    jnp.concatenate([rest, values[:, 128:]], axis=1),
                ],
                axis=0,
            )
            out = dot_nn(lhs, jnp.concatenate(probs[pair * 2 : pair * 2 + 2], axis=0))
            for j in range(2):
                for i in range(2):
                    attended[pair * 2 + j].append(
                        out[j * 32 + i * 16 : j * 32 + (i + 1) * 16, i * 128 : (i + 1) * 128]
                    )

    steps = [(half, t) for half in range(2) for t in range(4 // per_tile)]
    scores = scores_of(*steps[0])
    for k, step in enumerate(steps):
        yield
        ahead = scores_of(*steps[k + 1]) if k + 1 < len(steps) else None
        probs = []
        for j in range(4):
            probs.append(weights_of(scores[j * length : (j + 1) * length]))
            if length == 128:
                yield
        gather(*step, probs)
        yield
        scores = ahead
    yield
    lines = load()
    if length == 64:
        new = []
        for pair in range(2):
            joined = jnp.concatenate(attended[pair], axis=0).astype(BF16)
            update = dot_tn(joined, weights.out)
            new += [lines[pair * 2] + update[:64], lines[pair * 2 + 1] + update[64:]]
        return new
    return [
        lines[j] + dot_tn(jnp.concatenate(attended[j], axis=0).astype(BF16), weights.out)
        for j in range(4)
    ]


def label_of(occ_ref, group, tile_y, tile_z):
    label = jnp.int32(0)
    for k in range(1, GROUP):
        label = label + k * occ_ref[tile_y, tile_z, group * GROUP + k]
    return label


def tile_marks(occ_ref, group):
    index = lax.broadcasted_iota(jnp.int32, (1, 1, occ_ref.shape[2]), 2)
    return jnp.where(index // GROUP == group, occ_ref[...], 0).astype(F32)


def same_tile_mask(mask_ref, marks):
    marks = jnp.concatenate([jnp.broadcast_to(m, (TILE, m.shape[1])) for m in marks], axis=0)
    marks = marks.astype(BF16)
    mask_ref[...] = (dot_nt(marks[: mask_ref.shape[0]], marks) - 1.0) * BIG
    return lambda: jnp.concatenate([mask_ref[...]] * 2, axis=1)


def x_kernel(occ_ref, vol_ref, *refs):
    given, (out_ref, res_ref, starts_out) = refs[:5], refs[5:8]
    vin, whole, hs, done, starts, occ, sems, whole_sems, out_sems, table_sems = refs[8:18]
    weight_refs, weight_sems = refs[18:23], refs[23]
    chip, slab = lax.axis_index("chip"), lax.axis_index("slab")
    tile_y = chip // 2
    occ_load = pltpu.make_async_copy(occ_ref, occ, table_sems.at[1])
    occ_load.start()
    weight_loads = [
        pltpu.make_async_copy(given[0], weight_refs[0], weight_sems.at[0]),
        *[
            pltpu.make_async_copy(given[k].at[pl.ds(0, 1)], weight_refs[k], weight_sems.at[k])
            for k in range(1, 5)
        ],
    ]
    for copy in weight_loads:
        copy.start()
    occ_load.wait()
    tiles = []
    for g in range(4):
        start = (g * GROUP + label_of(occ, g, tile_y, slab)) * TILE
        starts[g : g + 1, :] = jnp.full((1, 128), start, jnp.int32)
        tiles.append(
            pltpu.make_async_copy(
                vol_ref.at[pl.ds(start, TILE)], vin.at[pl.ds(g * TILE, TILE)], sems.at[g]
            )
        )
    fetch = pltpu.make_async_copy(vol_ref, whole, whole_sems.at[0])
    store = pltpu.make_async_copy(whole, res_ref, whole_sems.at[1])
    for copy in tiles:
        copy.start()
    starts_copy = pltpu.make_async_copy(starts, starts_out, table_sems.at[0])
    starts_copy.start()
    for copy in weight_loads:
        copy.wait()
    weights = Weights(0, *weight_refs)
    for copy in tiles:
        copy.wait()
    fetch.start()
    outs = []
    held = hs.reshape(2, 64, STRIDE, 128)

    def load_quad(u):
        half = u // 8
        asked = []

        def load():
            if u % 8 == 0 and not asked:
                rows = vin[:, :, half * 8 : (half + 1) * 8, :].astype(F32)
                held[half, :, :32, :] = rows.reshape(64, 32, 128)
            if u == 15 and not asked:
                fetch.wait()
                store.start()
            asked.append(u)
            return [hs[place(u, j), :] for j in range(4)]

        return load

    def place(u, j):
        return pl.ds((u // 8) * 64 * STRIDE + (u % 8) * 4 + j, 64, stride=STRIDE)

    def finish(u, new):
        for j in range(4):
            hs[place(u, j), :] = new[j]
        if u % 8 == 7:
            half = u // 8
            done[half] = held[half, :, :32, :].astype(BF16)
            outs.append(pltpu.make_async_copy(done.at[half], out_ref.at[half], out_sems.at[half]))
            outs[-1].start()

    staggered([attend_quad(load_quad(u), weights) for u in range(16)], finish)
    for copy in [store, *outs, starts_copy]:
        copy.wait()


def y_kernel(occ_ref, in_ref, *refs):
    weight_refs, (keep_ref, send_low, send_high, hs) = refs[:5], refs[5:]
    core = lax.axis_index("core")
    held = hs.reshape(4, 16, 2, 4, Y_STRIDE, 128)
    for side in range(2):
        held[:, :, side, :, :8, :] = in_ref[side].astype(F32).reshape(4, 16, 4, 8, 128)
    weights = Weights(1, *weight_refs)
    marks = tile_marks(occ_ref, lax.axis_index("slab"))
    masks = [SpareLanes([marks[k, t : t + 1] for k in range(8)]) for t in range(4)]

    def place(u, j):
        return pl.ds((u // 2) * 128 * Y_STRIDE + (u % 2) * 4 + j, 128, stride=Y_STRIDE)

    def load_quad(u):
        return lambda: [hs[place(u, j), :] for j in range(4)]

    def finish(u, new):
        for j in range(4):
            hs[place(u, j), :] = new[j]
        if u % 2:
            k = u // 2
            for p in range(32):
                send_ref = send_low if k < 2 else send_high
                for ref, at, side in ((keep_ref, k, core), (send_ref, k % 2, 1 - core)):
                    rows = [held[k, p // 2, p % 2, side * 2 + j, :8, :] for j in range(2)]
                    ref[at, p] = jnp.concatenate(rows, axis=0).astype(BF16)

    staggered([attend_quad(load_quad(u), weights, masks[u // 2]) for u in range(8)], finish)


def z_kernel(occ_ref, kept_ref, got_low, got_high, *refs):
    weight_refs, (out_ref, mask_ref) = refs[:5], refs[5:]
    first = lax.axis_index("core") == 0
    weights = Weights(2, *weight_refs)

    marks = tile_marks(occ_ref, lax.axis_index("slab"))
    masks = [
        same_tile_mask(mask_ref.at[k], [marks[k, t : t + 1] for t in range(4)] * 2)
        for k in range(8)
    ]

    def load_quad(quad):
        lines = []

        def load():
            if not lines:
                for u in (quad * 2, quad * 2 + 1):
                    pair = ([], [])
                    for t in range(4):
                        got_ref = got_low if t < 2 else got_high
                        for ref, at in ((kept_ref, t), (got_ref, t % 2)):
                            both = ref[at, u].astype(F32)
                            pair[0].append(both[:8])
                            pair[1].append(both[8:])
                    lines.extend(jnp.concatenate(rows, axis=0) for rows in pair)
            return lines

        return load

    def finish(quad, new):
        for j in range(4):
            u = quad * 2 + j // 2
            for t in range(4):
                kept, got = new[j][t * 16 : t * 16 + 8], new[j][t * 16 + 8 : t * 16 + 16]
                ordered = jnp.concatenate(
                    [jnp.where(first, kept, got), jnp.where(first, got, kept)], axis=0
                )
                rows = slice((j % 2) * 16, (j % 2 + 1) * 16)
                out_ref[u % 2, t * 16 + u // 2, rows, :] = ordered.astype(BF16)

    staggered([attend_quad(load_quad(u), weights, masks[u // 2]) for u in range(16)], finish)


def merge_kernel(starts_ref, new_ref, res_in_ref, res_ref, sems):
    del res_in_ref
    starts = starts_ref[...]
    copies = []
    for g in range(4):
        start = pl.multiple_of(starts[g, 0], TILE)
        for side in range(2):
            copies.append(
                pltpu.make_async_copy(
                    new_ref.at[side, pl.ds(g * TILE, TILE)],
                    res_ref.at[pl.ds(start, TILE), pl.ds(side * 2, 2)],
                    sems.at[g * 2 + side],
                )
            )
            copies[-1].start()
    for copy in copies:
        copy.wait()


VMEM = pl.BlockSpec(memory_space=pltpu.VMEM)
ANY = pl.BlockSpec(memory_space=pl.ANY)
HBM = pl.BlockSpec(memory_space=pltpu.HBM)
PARAMS = pltpu.CompilerParams(vmem_limit_bytes=VMEM_BYTES)


def body(volume, occupancy, gains, w_query, w_key, w_value, w_out):
    params = (gains, w_query, w_key, w_value, w_out)
    occupancy = jnp.transpose(occupancy, (1, 2, 0))
    table = jax.ShapeDtypeStruct((8, 128), jnp.int32)
    after_x, copied, starts = pl.pallas_call(
        x_kernel,
        out_shape=(
            jax.ShapeDtypeStruct((2, 64, 32, 128), BF16),
            jax.ShapeDtypeStruct(volume.shape, BF16),
            table,
        ),
        in_specs=[HBM, HBM, *[HBM] * 5],
        out_specs=(HBM,) * 3,
        scratch_shapes=[
            pltpu.VMEM((64, 4, 16, 128), BF16),
            pltpu.VMEM(volume.shape, BF16),
            pltpu.VMEM((2 * 64 * STRIDE, 128), F32),
            pltpu.VMEM((2, 64, 32, 128), BF16),
            pltpu.VMEM(table.shape, table.dtype),
            pltpu.SMEM(occupancy.shape, jnp.int32),
            pltpu.SemaphoreType.DMA((4,)),
            pltpu.SemaphoreType.DMA((2,)),
            pltpu.SemaphoreType.DMA((2,)),
            pltpu.SemaphoreType.DMA((2,)),
            pltpu.VMEM(gains.shape, gains.dtype),
            *[pltpu.VMEM((1, *array.shape[1:]), array.dtype) for array in params[1:]],
            pltpu.SemaphoreType.DMA((5,)),
        ],
        compiler_params=pltpu.CompilerParams(vmem_limit_bytes=60 * 2**20),
        name="x_phase",
    )(occupancy, volume, *params)

    every = ("core", "slab", "chip")
    planes = lax.all_to_all(after_x.reshape(128, 32, 128), every, 0, 0, tiled=True)

    half = jax.ShapeDtypeStruct((4, 32, 16, 128), BF16)
    quarter = jax.ShapeDtypeStruct((2, 32, 16, 128), BF16)
    kept, *sent = pl.pallas_call(
        y_kernel,
        out_shape=(half, quarter, quarter),
        in_specs=[VMEM] * 7,
        out_specs=(VMEM, VMEM, VMEM),
        scratch_shapes=[pltpu.VMEM((4 * 128 * Y_STRIDE, 128), F32)],
        compiler_params=PARAMS,
        name="y_phase",
    )(occupancy, planes.reshape(2, 64, 32, 128), *params)

    got = [lax.ppermute(part, "core", [(0, 1), (1, 0)]) for part in sent]

    after_z = pl.pallas_call(
        z_kernel,
        out_shape=jax.ShapeDtypeStruct((2, 64, 32, 128), BF16),
        in_specs=[VMEM] * 9,
        out_specs=VMEM,
        scratch_shapes=[pltpu.VMEM((8, 64, 128), F32)],
        compiler_params=PARAMS,
        name="z_phase",
    )(occupancy, kept, *got, *params)

    home = lax.all_to_all(after_z.reshape(128, 32, 128), every, 0, 0, tiled=True)

    return pl.pallas_call(
        merge_kernel,
        out_shape=jax.ShapeDtypeStruct(volume.shape, BF16),
        in_specs=[VMEM, ANY, HBM],
        out_specs=HBM,
        scratch_shapes=[pltpu.SemaphoreType.DMA((8,))],
        input_output_aliases={2: 0},
        compiler_params=PARAMS,
        name="merge",
    )(starts, home.reshape(2, 64, 2, 16, 128), copied)


def solution(mesh):
    devices = mesh.devices.reshape(mesh.shape["slab"], -1, 2)
    cores = jax.sharding.Mesh(devices, ("slab", "chip", "core"))
    volume = P(None, ("chip", "core"), "slab", None)
    placed = (volume, P(), P(), P(), P(), P(), P())
    return jax.shard_map(body, mesh=cores, in_specs=placed, out_specs=volume, check_vma=False)
```
